128 devices in a mesh: zero: 8 (over y_hi, x), dp: 16 (over z, y_lo, core).
Axes of the slice: x: 4, y: 4 (y_hi: 2, y_lo: 2; y = y_hi * 2 + y_lo), z: 4, core: 2. Of those that a mesh axis runs over, the one named last changes fastest.
Arguments:
- hidden: bfloat16 [16, 1024, 8192], P('dp', 'zero'), may hold values from -6 to 6
- queries: bfloat16 [16, 1024, 4096], P('dp', 'zero'), may hold values from -400 to 400
- grad_out: bfloat16 [16, 1024, 4096], P('dp', 'zero'), may hold values from -6 to 6
- key_weight: bfloat16 [8192, 512], P(('zero', 'dp')), may hold values from -0.0625 to 0.0625
- value_weight: bfloat16 [8192, 512], P(('zero', 'dp')), may hold values from -0.0625 to 0.0625
- doc_lengths: int32 [16, 3], P('dp'), may hold values from 1 to 896, 1024 in all within a row
Outputs:
- d_queries: bfloat16 [16, 1024, 4096], P('dp', 'zero')
- d_hidden: bfloat16 [16, 1024, 8192], P('dp', 'zero')
- grad_key_weight: float32 [8192, 512], P(('zero', 'dp'))
- grad_value_weight: float32 [8192, 512], P(('zero', 'dp'))
The draws below stay inside these ranges and needn't reach their ends.
Inputs may be any that keep to these rules, and one draw needn't show every extreme that they name: `doc_lengths`: each row holds the lengths of 3 documents packed in order into one group of 1024 tokens, summing to 1024.
All inputs are finite; a program needn't handle non-finite values.
Results may differ from the reference program's by a relative error of at most 0.029.
The reference program's roundings to bfloat16 on the way count: a program that leaves them out, or rounds other values in their place, can miss the bound.
Values may be sent and summed in bfloat16 or wider, within the bound.
A program may use at most 128 MiB of HBM per device.

```python
import math
import jax
import jax.numpy as jnp
import numpy as np
from jax import lax

D = 8192
Q_HEADS = 32
KV_HEADS = 4
HD = 128
TOK_DEV = 128
DOCS = 3
GROUPS = 16
GROUP_TOKENS = 1024
MOST_DOC = 896
N_ZERO = 8


def draw_queries(key, part):
    key = jax.random.fold_in(key, 7)
    shape = (GROUPS, GROUP_TOKENS, Q_HEADS * HD)
    values = jnp.clip(jax.random.normal(key, shape, jnp.float32), -6.0, 6.0)
    return values.astype(jnp.bfloat16)


def level_of(stream_key, extent, pieces, smallest, top_value):
    def one(position, blocks):
        draws = jax.random.uniform(jax.random.fold_in(jax.random.fold_in(stream_key, 6), position), (blocks,), jnp.float32, smallest / len(pieces), top_value / len(pieces))
        return jnp.repeat(jnp.exp(draws), extent[position] // blocks).reshape((-1,) + (1,) * (len(extent) - position - 1))

    loudness = one(*pieces[0])
    for cut in pieces[1:]:
        loudness = loudness * one(*cut)
    return loudness


def profile(amount, total, bound, slope):
    loads = [(1 << 20) // math.isqrt(rank ** slope) + 1 for rank in range(2, amount + 1)]
    rest, counts = total - bound - (amount - 1), [1] * (amount - 1)
    while rest > 0:
        free = [i for i in range(amount - 1) if counts[i] < bound]
        mass, budget = sum([loads[i] for i in free]), rest
        for i in free:
            addition = min(bound - counts[i], max(1, budget * loads[i] // mass), rest)
            counts[i] = counts[i] + addition
            rest = rest - addition
    return np.array([bound] + counts)


def uneven(own_key, number_of, total, most, skew):
    if number_of == 2:
        one = jax.random.randint(own_key, (), max(1, total - most), min(most, total - 1) + 1)
        return jnp.stack([one, total - one])
    tallies = jnp.asarray(profile(number_of, total, most, skew), jnp.int32)
    pairs = (number_of - 1) // 2
    giver, taker = tallies[1:1 + 2 * pairs:2], tallies[2:2 + 2 * pairs:2]
    room = jnp.minimum(giver - 1, most - taker)
    shifted = jax.random.randint(jax.random.fold_in(own_key, 1), (pairs,), 0, 1 << 20) % (room + 1)
    tallies = tallies.at[1:1 + 2 * pairs:2].set(giver - shifted).at[2:2 + 2 * pairs:2].set(taker + shifted)
    return tallies[jax.random.permutation(jax.random.fold_in(own_key, 2), number_of)]


def scatter_about(own_key, extent, spread, limit, cuts=(), kind=jnp.bfloat16):
    values = jax.random.normal(own_key, extent, jnp.float32) * spread
    if len(cuts) > 0:
        values = level_of(own_key, extent, cuts, -0.22, 0.18) * values
    return jnp.clip(values, min=-limit, max=limit).astype(kind)


def setup_inputs(seed: int = 0) -> dict:
    key_list = jax.random.split(jax.random.key(seed), 7)
    hidden = scatter_about(key_list[0], (GROUPS, GROUP_TOKENS, D), 1.0, 6.0, ((0, 16), (1, 8)))
    queries = draw_queries(jax.random.fold_in(key_list[6], 71), 0)
    grad_out = scatter_about(key_list[2], (GROUPS, GROUP_TOKENS, Q_HEADS * HD), 1.0, 6.0, ((0, 16), (1, 8)))
    key_weight = scatter_about(key_list[3], (D, KV_HEADS * HD), D ** -0.5, 0.0625, ((0, 128),))
    value_weight = scatter_about(key_list[4], (D, KV_HEADS * HD), D ** -0.5, 0.0625, ((0, 128),))
    doc_lengths = jax.vmap(lambda own: uneven(own, DOCS, GROUP_TOKENS, MOST_DOC, 2))(jax.random.split(key_list[5], GROUPS)).reshape((GROUPS, DOCS)).astype(jnp.int32)
    return dict(hidden=hidden, queries=queries, grad_out=grad_out, key_weight=key_weight, value_weight=value_weight, doc_lengths=doc_lengths)


ROPE_BASE = 500000.0
NEGATIVE = -1.0e30
HIGHEST = lax.Precision.HIGHEST


def doc_layout(lengths, group_len):
    doc_ends = jnp.cumsum(lengths).astype(jnp.int32)
    places = jnp.arange(group_len, dtype=jnp.int32)
    passed = (doc_ends[None, :] <= places[:, None]).astype(jnp.int32)
    doc_ids = jnp.sum(passed, axis=1).astype(jnp.int32)
    before = jnp.sum(passed * lengths[None, :], axis=1).astype(jnp.int32)
    return doc_ids, places - before


def rope_tables(doc_pos, head_dim):
    half_dim = head_dim // 2
    inverse_freq = ROPE_BASE ** (-2.0 * jnp.arange(half_dim, dtype=jnp.float32) / head_dim)
    angles = doc_pos.astype(jnp.float32)[:, None] * inverse_freq[None, :]
    angles = jnp.concatenate([angles, angles], axis=1)
    return jnp.cos(angles), jnp.sin(angles)


def rotate(key_rows, cosine, sine_table, kv_heads):
    row_count = key_rows.shape[0]
    per_head = key_rows.reshape(row_count, kv_heads, -1)
    half_dim = per_head.shape[2] // 2
    turned = jnp.concatenate([-per_head[..., half_dim:], per_head[..., :half_dim]], axis=2)
    result = per_head * cosine[:, None, :] + turned * sine_table[:, None, :]
    return result.reshape(row_count, -1)


def unrotate(grad_rows, cosine, sine_table, kv_heads):
    row_count = grad_rows.shape[0]
    per_head = grad_rows.reshape(row_count, kv_heads, -1)
    half_dim = per_head.shape[2] // 2
    scaled = per_head * sine_table[:, None, :]
    moved_back = jnp.concatenate([scaled[..., half_dim:], -scaled[..., :half_dim]], axis=2)
    return (per_head * cosine[:, None, :] + moved_back).reshape(row_count, -1)


def rounded(value):
    return lax.optimization_barrier(value.astype(jnp.bfloat16)).astype(jnp.float32)


def attention_grads(queries, grad_out, key_rows, value_rows, query_doc, query_at, key_doc):
    row_count = queries.shape[0]
    key_count = key_rows.shape[0]
    head_dim = HD
    groups = Q_HEADS // KV_HEADS
    score_scale = head_dim ** -0.5
    query_heads = queries.astype(jnp.float32).reshape(row_count, KV_HEADS, groups, head_dim)
    grad_heads = grad_out.astype(jnp.float32).reshape(row_count, KV_HEADS, groups, head_dim)
    key_heads = key_rows.astype(jnp.float32).reshape(key_count, KV_HEADS, head_dim)
    value_heads = value_rows.astype(jnp.float32).reshape(key_count, KV_HEADS, head_dim)
    key_at = jnp.arange(key_count, dtype=jnp.int32)
    allowed = (query_doc[:, None] == key_doc[None, :]) & (query_at[:, None] >= key_at[None, :])
    scores = jnp.einsum("tkgd,skd->kgts", query_heads, key_heads, precision=HIGHEST) * score_scale
    running_max = jnp.max(jnp.where(allowed, scores, NEGATIVE), axis=-1)
    summed = jnp.sum(jnp.where(allowed, jnp.exp(scores - running_max[..., None]), 0.0), axis=-1)
    log_total = running_max + jnp.log(summed)
    weights = jnp.where(allowed, jnp.exp(scores - log_total[..., None]), 0.0)
    weights_low = rounded(weights)
    attended = jnp.einsum("kgts,skd->kgtd", weights_low, value_heads, precision=HIGHEST)
    delta = jnp.einsum("tkgd,kgtd->kgt", grad_heads, attended, precision=HIGHEST)
    dvalue_part = jnp.einsum("kgts,tkgd->skd", weights_low, grad_heads, precision=HIGHEST)
    dweights = jnp.einsum("tkgd,skd->kgts", grad_heads, value_heads, precision=HIGHEST)
    dscores = rounded(weights * (dweights - delta[..., None]))
    dquery = jnp.einsum("kgts,skd->tkgd", dscores, key_heads, precision=HIGHEST) * score_scale
    dkey_part = jnp.einsum("kgts,tkgd->skd", dscores, query_heads, precision=HIGHEST) * score_scale
    return dquery.reshape(row_count, -1), dkey_part.reshape(key_count, -1), dvalue_part.reshape(key_count, -1)


def reference(hidden, queries, grad_out, key_weight, value_weight, doc_lengths):
    kv_width = KV_HEADS * HD

    def one_group(state_in, slices):
        rows_in, query_in, grad_in, lengths = slices
        doc_ids, doc_pos = doc_layout(lengths, GROUP_TOKENS)
        cosine, sine_table = rope_tables(doc_pos, HD)
        key_rows = rotate(jnp.dot(rows_in, key_weight, preferred_element_type=jnp.float32), cosine, sine_table, KV_HEADS).astype(jnp.bfloat16)
        value_rows = jnp.dot(rows_in, value_weight, preferred_element_type=jnp.float32).astype(jnp.bfloat16)

        def one_block(number):
            offset = number * TOK_DEV
            query_block = lax.dynamic_slice_in_dim(query_in, offset, TOK_DEV, 0)
            grad_block = lax.dynamic_slice_in_dim(grad_in, offset, TOK_DEV, 0)
            query_doc = lax.dynamic_slice_in_dim(doc_ids, offset, TOK_DEV, 0)
            query_at = (offset + jnp.arange(TOK_DEV, dtype=jnp.int32)).astype(jnp.int32)
            dquery, dkey_part, dvalue_part = attention_grads(query_block, grad_block, key_rows, value_rows, query_doc, query_at, doc_ids)
            return dquery.astype(jnp.bfloat16), rounded(dkey_part), rounded(dvalue_part)

        dquery_blocks, dkey_parts, dvalue_parts = lax.map(one_block, jnp.arange(N_ZERO, dtype=jnp.int32))
        dkeys = jnp.sum(dkey_parts, axis=0)
        dvalues = jnp.sum(dvalue_parts, axis=0)
        dkeys_pre = unrotate(dkeys, cosine, sine_table, KV_HEADS).astype(jnp.bfloat16)
        dvalues_low = dvalues.astype(jnp.bfloat16)
        dhidden = jnp.dot(dkeys_pre, key_weight.T, preferred_element_type=jnp.float32) + jnp.dot(dvalues_low, value_weight.T, preferred_element_type=jnp.float32)
        rows_split = rows_in.astype(jnp.float32).reshape(N_ZERO, TOK_DEV, D)
        key_split = dkeys_pre.astype(jnp.float32).reshape(N_ZERO, TOK_DEV, kv_width)
        value_split = dvalues_low.astype(jnp.float32).reshape(N_ZERO, TOK_DEV, kv_width)
        key_terms = jnp.einsum("ntd,ntk->ndk", rows_split, key_split, precision=HIGHEST)
        value_terms = jnp.einsum("ntd,ntk->ndk", rows_split, value_split, precision=HIGHEST)
        grad_key = state_in[0] + jnp.sum(rounded(key_terms), axis=0)
        grad_value = state_in[1] + jnp.sum(rounded(value_terms), axis=0)
        dquery_all = dquery_blocks.reshape(GROUP_TOKENS, Q_HEADS * HD)
        return (grad_key, grad_value), (dquery_all, dhidden.astype(jnp.bfloat16))

    initial = (jnp.zeros((D, kv_width), jnp.float32), jnp.zeros((D, kv_width), jnp.float32))
    grads_out, stacked = lax.scan(one_group, initial, (hidden, queries, grad_out, doc_lengths))
    return stacked[0], stacked[1], grads_out[0], grads_out[1]
```

```python
import functools

import jax
import jax.numpy as jnp
from jax import lax
from jax.experimental import pallas as pl
from jax.experimental.pallas import tpu as pltpu
from jax.sharding import PartitionSpec as P

KV_HEADS = 4
HD = 128
ROPE_BASE = 500000.0
NEGATIVE = -1e30
LOG2E = 1.4426950408889634
MESH = pl.DeviceIdType.MESH
TOK = 128
WIDE = 8192
ANY = pl.BlockSpec(memory_space=pl.ANY)
VMEM = pl.BlockSpec(memory_space=pltpu.VMEM)
BF = jnp.bfloat16
F32 = jnp.float32


def doc_layout(lengths, group_len):
    doc_ends = jnp.cumsum(lengths)
    places = jnp.arange(group_len, dtype=jnp.int32)
    passed = (doc_ends[None, :] <= places[:, None]).astype(jnp.int32)
    doc_ids = jnp.sum(passed, axis=1)
    before = jnp.sum(passed * lengths[None, :], axis=1)
    return (doc_ids, places - before)


def rope_tables(doc_pos, head_dim):
    half_dim = head_dim // 2
    inverse_freq = ROPE_BASE ** (-2.0 * jnp.arange(half_dim, dtype=jnp.float32) / head_dim)
    angles = doc_pos.astype(jnp.float32)[:, None] * inverse_freq[None, :]
    angles = jnp.concatenate([angles, angles], axis=1)
    return (jnp.cos(angles), jnp.sin(angles))


def rotate(key_rows, cosine, sine_table, kv_heads):
    row_count = key_rows.shape[0]
    per_head = key_rows.reshape(row_count, kv_heads, -1)
    half_dim = per_head.shape[2] // 2
    turned = jnp.concatenate([-per_head[..., half_dim:], per_head[..., :half_dim]], axis=2)
    return per_head * cosine[:, None, :] + turned * sine_table[:, None, :]


def place():
    j, i = lax.axis_index("zero"), lax.axis_index("dp")
    return j // 4, j % 4, i // 4, (i // 2) % 2, i % 2


def device(u, x, z, w, c):
    return (u * 4 + x, z * 4 + w * 2 + c)


class Peers:
    def __init__(self):
        self.u, self.x, self.z, self.w, self.c = place()

    def along_x(self, d):
        return device(self.u, (self.x + d) % 4, self.z, self.w, self.c)

    def along_z(self, d):
        return device(self.u, self.x, (self.z + d) % 4, self.w, self.c)

    def y_at(self, d):
        y = (2 * self.u + self.w + d) % 4
        return y // 2, y % 2

    def along_y(self, d):
        u, w = self.y_at(d)
        return device(u, self.x, self.z, w, self.c)

    def in_group(self, du, dx):
        return device((self.u + du) % 2, (self.x + dx) % 4, self.z, self.w, self.c)

    def on_plane(self, dy, dx):
        u, w = self.y_at(dy)
        return device(u, (self.x + dx) % 4, self.z, w, self.c)

    def sibling(self):
        return device(self.u, self.x, self.z, self.w, 1 - self.c)


def meet(devices):
    barrier = pltpu.get_barrier_semaphore()
    for one in devices:
        pl.semaphore_signal(barrier, inc=1, device_id=one, device_id_type=MESH)
    pl.semaphore_wait(barrier, len(devices))


class Copies:
    def __init__(self, send, recv):
        self.send, self.recv, self.used = send, recv, 0

    def make(self, src, dst, to):
        at = self.used
        self.used += 1
        return pltpu.make_async_remote_copy(
            src_ref=src,
            dst_ref=dst,
            send_sem=self.send.at[at],
            recv_sem=self.recv.at[at],
            device_id=to,
            device_id_type=MESH,
        )

    def start(self, src, dst, to):
        copy = self.make(src, dst, to)
        copy.start()
        return copy


GROUP = [(du, dx) for du in (1, 0) for dx in (2, 1, 3, 0)][:-1]
PLANE = [(dy, dx) for dy in (2, 1, 3, 0) for dx in (2, 1, 3, 0)][:-1]
STEPS = (2, 1, 3)


def comm_call(kernel, number, outs, in_specs, out_specs, remote, local, scratch=()):
    return pl.pallas_call(
        kernel,
        out_shape=outs,
        in_specs=in_specs,
        out_specs=out_specs,
        scratch_shapes=[
            pltpu.SemaphoreType.DMA((remote,)),
            pltpu.SemaphoreType.DMA((remote,)),
            pltpu.SemaphoreType.DMA((local,)),
            *scratch,
        ],
        compiler_params=pltpu.CompilerParams(
            collective_id=number, has_side_effects=True, vmem_limit_bytes=48 << 20
        ),
    )


def spread_kernel(hidden, query, wkey, wvalue, hid_g, wk, wv, q_h, send, recv, here):
    p = Peers()
    u, x, z, w, c = p.u, p.x, p.z, p.w, p.c
    cp = Copies(send, recv)
    local = [
        pltpu.make_async_copy(wkey, wk.at[u, x, w, c], here.at[0]),
        pltpu.make_async_copy(wvalue, wv.at[u, x, w, c], here.at[1]),
        pltpu.make_async_copy(
            query.at[:, pl.ds(pl.multiple_of(x * 1024, 1024), 1024)], q_h.at[x], here.at[2]
        ),
    ]
    for one in local:
        one.start()
    own_pieces = []
    for piece in range(8):
        start = pl.multiple_of((piece * 4 + z) * 256, 256)
        own_pieces.append(
            pltpu.make_async_copy(
                hidden.at[:, pl.ds(start, 256)],
                hid_g.at[z, :, pl.ds(piece * 256, 256)],
                here.at[3 + piece],
            )
        )
        own_pieces[-1].start()
    meet(
        [p.along_x(d) for d in STEPS]
        + [p.along_y(d) for d in STEPS]
        + [p.along_z(d) for d in STEPS]
        + [p.sibling()]
    )
    key_y = [cp.start(wkey, wk.at[u, x, w, c], p.along_y(d)) for d in STEPS]
    value_x = [cp.start(wvalue, wv.at[u, x, w, c], p.along_x(d)) for d in STEPS]
    whole = []
    for d in STEPS:
        there = (z + d) % 4
        at = cp.used
        for piece in range(8):
            start = pl.multiple_of((piece * 4 + there) * 256, 256)
            cp.used = at
            cp.start(
                hidden.at[:, pl.ds(start, 256)],
                hid_g.at[z, :, pl.ds(piece * 256, 256)],
                p.along_z(d),
            )
        cp.used = at
        came = (z + 4 - d) % 4
        whole.append(cp.make(hid_g.at[came], hid_g.at[came], p.along_z(d)))
    local[0].wait()
    for one in key_y:
        one.wait_recv()
    column = wk.at[:, x, :, c]
    key_x = [cp.start(column, column, p.along_x(d)) for d in STEPS]
    to_core = [cp.start(column, column, p.sibling())]
    local[1].wait()
    for one in value_x:
        one.wait_recv()
    row = wv.at[u, :, w, c]
    value_y = [cp.start(row, row, p.along_y(d)) for d in STEPS]
    to_core.append(cp.start(row, row, p.sibling()))
    sent_q = []
    for d in STEPS:
        there = (x + d) % 4
        start = pl.multiple_of(there * 1024, 1024)
        sent_q.append(cp.start(query.at[:, pl.ds(start, 1024)], q_h.at[x], p.along_x(d)))
    for d, one in zip((1, 3, 2), (key_x[1], key_x[2], key_x[0])):
        one.wait_recv()
        column = wk.at[:, (x + 4 - d) % 4, :, c]
        to_core.append(cp.start(column, column, p.sibling()))
    for d, one in zip((1, 3, 2), (value_y[1], value_y[2], value_y[0])):
        one.wait_recv()
        from_u, from_w = p.y_at(4 - d)
        row = wv.at[from_u, :, from_w, c]
        to_core.append(cp.start(row, row, p.sibling()))
    for one in to_core + sent_q + whole:
        one.wait_recv()
    for one in key_y + value_x + key_x + value_y + to_core + sent_q + whole:
        one.wait_send()
    for one in local[2:] + own_pieces:
        one.wait()


def spread(hidden, query, wkey, wvalue):
    shape = jax.ShapeDtypeStruct
    return comm_call(
        spread_kernel,
        0,
        (
            shape((4, TOK, 2048), BF),
            shape((2, 4, 2, 2, 64, 512), BF),
            shape((2, 4, 2, 2, 64, 512), BF),
            shape((4, TOK, 1024), BF),
        ),
        [ANY] * 4,
        (ANY,) * 4,
        26,
        11,
    )(hidden, query, wkey, wvalue)


def partials_kernel(kp, vp, grad, k_in, v_in, go_h, send, recv, here):
    p = Peers()
    x, z = p.x, p.z
    cp = Copies(send, recv)
    own = [
        pltpu.make_async_copy(kp.at[z], k_in.at[z], here.at[0]),
        pltpu.make_async_copy(vp.at[z], v_in.at[z], here.at[1]),
        pltpu.make_async_copy(
            grad.at[:, pl.ds(pl.multiple_of(x * 1024, 1024), 1024)], go_h.at[x], here.at[2]
        ),
    ]
    for one in own:
        one.start()
    meet([p.along_x(d) for d in STEPS] + [p.along_z(d) for d in STEPS])
    sent = []
    for d in STEPS:
        there = (z + d) % 4
        sent.append(cp.start(kp.at[there], k_in.at[z], p.along_z(d)))
        sent.append(cp.start(vp.at[there], v_in.at[z], p.along_z(d)))
    for d in STEPS:
        start = pl.multiple_of(((x + d) % 4) * 1024, 1024)
        sent.append(cp.start(grad.at[:, pl.ds(start, 1024)], go_h.at[x], p.along_x(d)))
    for one in sent:
        one.wait()
    for one in own:
        one.wait()


def partials(kp, vp, grad):
    shape = jax.ShapeDtypeStruct
    return comm_call(
        partials_kernel,
        1,
        (shape((4, TOK, 512), F32), shape((4, TOK, 512), BF), shape((4, TOK, 1024), BF)),
        [ANY] * 3,
        (ANY,) * 3,
        9,
        3,
    )(kp, vp, grad)


def heads_kernel(kv, kv_h, send, recv, here):
    p = Peers()
    u, x = p.u, p.x
    cp = Copies(send, recv)

    def head(at):
        return kv.at[:, pl.ds(pl.multiple_of(at * 256, 256), 256)]

    own = pltpu.make_async_copy(head(x), kv_h.at[u, x], here.at[0])
    own.start()
    meet([p.in_group(du, dx) for du, dx in GROUP])
    sent = [
        cp.start(head((x + dx) % 4), kv_h.at[u, x], p.in_group(du, dx)) for du, dx in GROUP
    ]
    for one in sent:
        one.wait()
    own.wait()


def heads(kv):
    shape = jax.ShapeDtypeStruct
    return comm_call(
        heads_kernel, 2, shape((2, 4, TOK, 256), BF), [ANY], ANY, 7, 1
    )(kv)


ROWS = 256


def attend_kernel(u_ref, low_ref, q, go, kv, dq, dkv, bias, kt, dk_sum, dv_sum):
    block, head = pl.program_id(0), pl.program_id(1)
    u = u_ref[0]
    scale = HD**-0.5

    @pl.when((block == 0) & (head == 0))
    def _():
        dk_sum[...] = jnp.zeros_like(dk_sum)
        dv_sum[...] = jnp.zeros_like(dv_sum)
        kt[...] = kv[:, :HD].astype(F32).T.astype(BF)

    @pl.when(head == 0)
    def _():
        key_at = lax.broadcasted_iota(jnp.int32, (1024, ROWS), 0)
        query_at = (u * 2 + block) * ROWS + lax.broadcasted_iota(jnp.int32, (1024, ROWS), 1)
        allowed = (key_at <= query_at) & (key_at >= low_ref[...])
        bias[...] = jnp.where(allowed, 0.0, NEGATIVE)

    def work(keys):
        query, grad = q[...], go[...]
        key, value = kv[:keys, :HD], kv[:keys, HD:]
        contract = (((1,), (1,)), ((), ()))
        s = lax.dot_general(key, query, contract, preferred_element_type=F32) + bias[:keys]
        top = jnp.max(s, axis=0, keepdims=True)
        e = jnp.exp2((s - top) * (scale * LOG2E))
        weights = e * (1.0 / jnp.sum(e, axis=0, keepdims=True))
        low = weights.astype(BF)
        dw = lax.dot_general(value, grad, contract, preferred_element_type=F32)
        delta = jnp.sum(low.astype(F32) * dw, axis=0, keepdims=True)
        ds = (weights * (dw - delta)).astype(BF)
        dv_sum[:keys] += jnp.dot(low, grad, preferred_element_type=F32)
        dk_sum[:keys] += jnp.dot(ds, query, preferred_element_type=F32)
        turned = jnp.dot(kt[:, :keys], ds, preferred_element_type=F32)
        dq[...] = (turned.T * scale).astype(BF)

    for count in range(1, 5):
        pl.when(u * 2 + block == count - 1)(functools.partial(work, count * ROWS))

    @pl.when((block == 1) & (head == 7))
    def _():
        dkv[:, :HD] = (dk_sum[...] * scale).astype(BF)
        dkv[:, HD:] = dv_sum[...].astype(BF)


def attend(u, low, q_h, go_h, kv_h):
    shape = jax.ShapeDtypeStruct
    one_head = pl.BlockSpec((ROWS, HD), lambda i, g, *_: (i, g))
    whole = pl.BlockSpec((1024, 256), lambda i, g, *_: (0, 0))
    return pl.pallas_call(
        attend_kernel,
        grid_spec=pltpu.PrefetchScalarGridSpec(
            num_scalar_prefetch=1,
            grid=(2, 8),
            in_specs=[
                pl.BlockSpec((1, ROWS), lambda i, g, *_: (0, i)),
                one_head,
                one_head,
                whole,
            ],
            out_specs=[one_head, whole],
            scratch_shapes=[
                pltpu.VMEM((1024, ROWS), F32),
                pltpu.VMEM((HD, 1024), BF),
                pltpu.VMEM((1024, HD), F32),
                pltpu.VMEM((1024, HD), F32),
            ],
        ),
        out_shape=[shape((512, 1024), BF), shape((1024, 256), BF)],
        compiler_params=pltpu.CompilerParams(vmem_limit_bytes=48 << 20),
    )(u, low, q_h, go_h, kv_h)


def collect_kernel(dkv, dq_h, cosine, sine, dkv_g, dq, send, recv, here, came, own_rows):
    p = Peers()
    u, x, z = p.u, p.x, p.z
    cp = Copies(send, recv)

    def head(at):
        return dq.at[:, pl.ds(pl.multiple_of(at * 1024, 1024), 1024)]

    own = [
        pltpu.make_async_copy(dkv.at[u, x], came.at[u, x], here.at[0]),
        pltpu.make_async_copy(dq_h.at[x], head(x), here.at[1]),
    ]
    for one in own:
        one.start()
    meet([p.in_group(du, dx) for du, dx in GROUP] + [p.along_z(d) for d in STEPS])
    sent = [
        cp.start(dkv.at[(u + du) % 2, (x + dx) % 4], came.at[u, x], p.in_group(du, dx))
        for du, dx in GROUP
    ]
    sent_q = [cp.start(dq_h.at[(x + d) % 4], head(x), p.along_x(d)) for d in STEPS]
    for one in sent:
        one.wait_recv()
    own[0].wait()
    cos, sin = cosine[...], sine[...]
    for h in range(KV_HEADS):
        total = came[0, h].astype(F32) + came[1, h].astype(F32)
        dk = total[:, :HD]
        scaled = dk * sin
        half = HD // 2
        back = jnp.concatenate([scaled[:, half:], -scaled[:, :half]], axis=1)
        own_rows[:, h * HD : (h + 1) * HD] = (dk * cos + back).astype(BF)
        own_rows[:, 512 + h * HD : 512 + (h + 1) * HD] = total[:, HD:].astype(BF)
    keep = pltpu.make_async_copy(own_rows, dkv_g.at[z], here.at[2])
    keep.start()
    sent_z = [cp.start(own_rows, dkv_g.at[z], p.along_z(d)) for d in STEPS]
    for one in sent_z + sent_q:
        one.wait_recv()
    for one in sent + sent_z + sent_q:
        one.wait_send()
    own[1].wait()
    keep.wait()


def collect(dkv, dq_h, cosine, sine):
    shape = jax.ShapeDtypeStruct
    return comm_call(
        collect_kernel,
        3,
        (shape((4, TOK, 1024), BF), shape((TOK, 4096), BF)),
        [ANY, ANY, VMEM, VMEM],
        (ANY, ANY),
        13,
        3,
        (pltpu.VMEM((2, 4, TOK, 256), BF), pltpu.VMEM((TOK, 1024), BF)),
    )(dkv, dq_h, cosine, sine)


def finish_kernel(dh, gw, dhidden, terms, send, recv, here, mine, other):
    p = Peers()
    u, x, z, w, c = p.u, p.x, p.z, p.w, p.c
    cp = Copies(send, recv)
    order = PLANE + [(0, 0)]
    loads = []
    for k, (dy, dx) in enumerate(order):
        tu, tw = p.y_at(dy)
        loads.append(
            pltpu.make_async_copy(gw.at[tu, (x + dx) % 4, tw, c], mine.at[k], here.at[k])
        )
        loads[-1].start()
    own_pieces = []
    for piece in range(8):
        start = pl.multiple_of((piece * 4 + z) * 256, 256)
        own_pieces.append(
            pltpu.make_async_copy(
                dh.at[z, :, pl.ds(piece * 256, 256)],
                dhidden.at[:, pl.ds(start, 256)],
                here.at[16 + piece],
            )
        )
        own_pieces[-1].start()
    meet(
        [p.on_plane(dy, dx) for dy, dx in PLANE]
        + [p.along_z(d) for d in STEPS]
        + [p.sibling()]
    )
    swapped = []
    for k, (dy, dx) in enumerate(order):
        tu, tw = p.y_at(dy)
        swapped.append(
            cp.start(gw.at[tu, (x + dx) % 4, tw, 1 - c], other.at[k], p.sibling())
        )
    whole = []
    for d in STEPS:
        there = (z + d) % 4
        at = cp.used
        for piece in range(8):
            start = pl.multiple_of((piece * 4 + z) * 256, 256)
            cp.used = at
            cp.start(
                dh.at[there, :, pl.ds(piece * 256, 256)],
                dhidden.at[:, pl.ds(start, 256)],
                p.along_z(d),
            )
        cp.used = at
        whole.append(cp.make(dh.at[there], dh.at[there], p.along_z(d)))
    sent = []
    for k, (dy, dx) in enumerate(order):
        loads[k].wait()
        swapped[k].wait_recv()
        mine[k] = (mine[k].astype(F32) + other[k].astype(F32)).astype(BF)
        if (dy, dx) == (0, 0):
            keep = pltpu.make_async_copy(mine.at[k], terms.at[k], here.at[24])
            keep.start()
        else:
            sent.append(cp.start(mine.at[k], terms.at[k], p.on_plane(dy, dx)))
    for one in sent + whole:
        one.wait_recv()
    for one in sent + whole + swapped:
        one.wait_send()
    for one in own_pieces:
        one.wait()
    keep.wait()


def finish(dh, gw):
    shape = jax.ShapeDtypeStruct
    return comm_call(
        finish_kernel,
        4,
        (shape((TOK, WIDE), BF), shape((16, 64, 1024), BF)),
        [ANY, ANY],
        (ANY, ANY),
        34,
        25,
        (pltpu.VMEM((16, 64, 1024), BF), pltpu.VMEM((16, 64, 1024), BF)),
    )(dh, gw)


def local(hidden, queries, grad_out, key_weight, value_weight, doc_lengths):
    lengths = doc_lengths[0]
    doc_ids, doc_pos = doc_layout(lengths, 1024)
    zero = lax.axis_index("zero")
    half = zero // 4
    my_pos = lax.dynamic_slice_in_dim(doc_pos, zero * TOK, TOK, 0)
    cosine, sine = rope_tables(my_pos, HD)
    first_key = jnp.arange(1024, dtype=jnp.int32) - doc_pos
    low = lax.dynamic_slice_in_dim(first_key, half * 512, 512, 0)[None, :]

    hid_g, wk, wv, q_h = spread(hidden[0], queries[0], key_weight, value_weight)
    hid_g = hid_g.reshape(512, 2048)
    wk, wv = wk.reshape(2048, 512), wv.reshape(2048, 512)
    kp = jnp.dot(hid_g, wk, preferred_element_type=F32).reshape(4, TOK, 512)
    vp = jnp.dot(hid_g, wv, preferred_element_type=F32).astype(BF).reshape(4, TOK, 512)
    k_in, v_in, go_h = partials(kp, vp, grad_out[0])
    k_rows = rotate(jnp.sum(k_in, axis=0), cosine, sine, KV_HEADS)
    v_rows = jnp.sum(v_in.astype(F32), axis=0).reshape(TOK, KV_HEADS, HD)
    kv = jnp.concatenate([k_rows, v_rows], axis=2).astype(BF).reshape(TOK, 1024)
    kv_h = heads(kv).reshape(1024, 256)
    dq_h, dkv = attend(
        half.astype(jnp.int32)[None], low, q_h.reshape(512, 1024), go_h.reshape(512, 1024), kv_h
    )
    dkv_g, dquery = collect(
        dkv.reshape(2, 4, TOK, 256), dq_h.reshape(4, TOK, 1024), cosine, sine
    )
    dkv_g = dkv_g.reshape(512, 1024)
    dh = jnp.dot(dkv_g[:, :512], wk.T, preferred_element_type=F32) + jnp.dot(
        dkv_g[:, 512:], wv.T, preferred_element_type=F32
    )
    gw = jnp.dot(hid_g.T, dkv_g, preferred_element_type=F32).astype(BF)
    dhidden, terms = finish(
        dh.astype(BF).reshape(4, TOK, 2048), gw.reshape(2, 4, 2, 2, 64, 1024)
    )
    grads = jnp.sum(terms.astype(F32), axis=0)
    return dquery[None], dhidden[None], grads[:, :512], grads[:, 512:]


def solution(mesh):
    return jax.shard_map(
        local,
        mesh=mesh,
        in_specs=(
            P("dp", "zero", None),
            P("dp", "zero", None),
            P("dp", "zero", None),
            P(("zero", "dp"), None),
            P(("zero", "dp"), None),
            P("dp", None),
        ),
        out_specs=(
            P("dp", "zero", None),
            P("dp", "zero", None),
            P(("zero", "dp"), None),
            P(("zero", "dp"), None),
        ),
        check_vma=False,
    )
```

```python
import functools

import jax
import jax.numpy as jnp
from jax import lax
from jax.experimental import pallas as pl
from jax.experimental.pallas import tpu as pltpu
from jax.sharding import PartitionSpec as P

KV_HEADS = 4
HD = 128
ROPE_BASE = 500000.0
NEGATIVE = -1e30
LOG2E = 1.4426950408889634
MESH = pl.DeviceIdType.MESH
TOK = 128
WIDE = 8192
ANY = pl.BlockSpec(memory_space=pl.ANY)
VMEM = pl.BlockSpec(memory_space=pltpu.VMEM)
BF = jnp.bfloat16
F32 = jnp.float32


def own_tables(lengths, offset):
    at = offset + lax.broadcasted_iota(jnp.int32, (TOK, HD), 0)
    first, second = lengths[0], lengths[0] + lengths[1]
    begin = jnp.where(at >= second, second, jnp.where(at >= first, first, 0))
    lane = lax.broadcasted_iota(jnp.int32, (TOK, HD), 1)
    frequency = ROPE_BASE ** (-2.0 * (lane % (HD // 2)).astype(F32) / HD)
    angles = (at - begin).astype(F32) * frequency
    return jnp.cos(angles), jnp.where(lane < HD // 2, -1.0, 1.0) * jnp.sin(angles)


def place():
    j, i = lax.axis_index("zero"), lax.axis_index("dp")
    return j // 4, j % 4, i // 4, (i // 2) % 2, i % 2


def device(u, x, z, w, c):
    return (u * 4 + x, z * 4 + w * 2 + c)


class Peers:
    def __init__(self):
        self.u, self.x, self.z, self.w, self.c = place()

    def along_x(self, d):
        return device(self.u, (self.x + d) % 4, self.z, self.w, self.c)

    def along_z(self, d):
        return device(self.u, self.x, (self.z + d) % 4, self.w, self.c)

    def y_at(self, d):
        y = (2 * self.u + self.w + d) % 4
        return y // 2, y % 2

    def along_y(self, d):
        u, w = self.y_at(d)
        return device(u, self.x, self.z, w, self.c)

    def in_group(self, du, dx):
        return device((self.u + du) % 2, (self.x + dx) % 4, self.z, self.w, self.c)

    def on_plane(self, dy, dx):
        u, w = self.y_at(dy)
        return device(u, (self.x + dx) % 4, self.z, w, self.c)

    def sibling(self):
        return device(self.u, self.x, self.z, self.w, 1 - self.c)


def meet(devices):
    barrier = pltpu.get_barrier_semaphore()
    for one in devices:
        pl.semaphore_signal(barrier, inc=1, device_id=one, device_id_type=MESH)
    pl.semaphore_wait(barrier, len(devices))


class Copies:
    def __init__(self, send, recv):
        self.send, self.recv, self.used = send, recv, 0

    def make(self, src, dst, to):
        at = self.used
        self.used += 1
        return pltpu.make_async_remote_copy(
            src_ref=src,
            dst_ref=dst,
            send_sem=self.send.at[at],
            recv_sem=self.recv.at[at],
            device_id=to,
            device_id_type=MESH,
        )

    def start(self, src, dst, to):
        copy = self.make(src, dst, to)
        copy.start()
        return copy


GROUP = [(du, dx) for du in (1, 0) for dx in (2, 1, 3, 0)][:-1]
PLANE = [(dy, dx) for dy in (2, 1, 3, 0) for dx in (2, 1, 3, 0)][:-1]
STEPS = (1, 3, 2)


def comm_call(kernel, number, outs, in_specs, out_specs, remote, local, scratch=()):
    return pl.pallas_call(
        kernel,
        out_shape=outs,
        in_specs=in_specs,
        out_specs=out_specs,
        scratch_shapes=[
            pltpu.SemaphoreType.DMA((remote,)),
            pltpu.SemaphoreType.DMA((remote,)),
            pltpu.SemaphoreType.DMA((local,)),
            *scratch,
        ],
        compiler_params=pltpu.CompilerParams(
            collective_id=number, has_side_effects=True, vmem_limit_bytes=60 << 20
        ),
    )


def lanes(at, size):
    return pl.ds(pl.multiple_of(at * size, size), size)


def turn(rows):
    return pltpu.roll(rows, HD // 2, 1)


def forward_kernel(
    hidden, query, grad, wkey, wvalue, cosine, sine,
    hid_out, wk_out, wv_out, q_h, go_h, kv_h,
    send, recv, here, hid, wk, wv, k_part, v_part, k_in, v_in, k_own, v_own, kv,
):
    p = Peers()
    u, x, z, w, c = p.u, p.x, p.z, p.w, p.c
    cp = Copies(send, recv)
    used = [0]

    def move(src, dst):
        copy = pltpu.make_async_copy(src, dst, here.at[used[0]])
        used[0] += 1
        copy.start()
        return copy

    own_key = move(wkey, wk.at[u, x, w, c])
    own_value = move(wvalue, wv.at[u, x, w, c])
    own_hidden = [
        move(hidden.at[:, lanes(piece * 4 + z, 256)], hid.at[z, :, pl.ds(piece * 256, 256)])
        for piece in range(8)
    ]
    later = [
        move(query.at[:, lanes(x, 1024)], q_h.at[x]),
        move(grad.at[:, lanes(x, 1024)], go_h.at[x]),
    ]
    meet(
        [p.along_z(d) for d in STEPS]
        + [p.on_plane(dy, 0) for dy in STEPS]
        + [p.on_plane(0, dx) for dx in STEPS]
        + [p.on_plane(2, dx) for dx in STEPS]
        + [p.sibling()]
    )
    key_y = [cp.start(wkey, wk.at[u, x, w, c], p.along_y(d)) for d in STEPS]
    value_x = [cp.start(wvalue, wv.at[u, x, w, c], p.along_x(d)) for d in STEPS]
    whole = []
    for d in STEPS:
        there, at = (z + d) % 4, cp.used
        for piece in range(8):
            cp.used = at
            cp.start(
                hidden.at[:, lanes(piece * 4 + there, 256)],
                hid.at[z, :, pl.ds(piece * 256, 256)],
                p.along_z(d),
            )
        cp.used = at
        came = (z + 4 - d) % 4
        whole.append(cp.make(hid.at[came], hid.at[came], p.along_z(d)))
    own_key.wait()
    for one in key_y:
        one.wait_recv()
    column = wk.at[:, x, :, c]
    key_x = [cp.start(column, column, p.along_x(d)) for d in STEPS]
    to_core = [cp.start(column, column, p.sibling())]
    own_value.wait()
    for one in value_x:
        one.wait_recv()
    row = wv.at[u, :, w, c]
    value_y = [cp.start(row, row, p.along_y(d)) for d in STEPS]
    to_core.append(cp.start(row, row, p.sibling()))
    sent = []
    for source, target in ((query, q_h), (grad, go_h)):
        for d in STEPS:
            sent.append(
                cp.start(source.at[:, lanes((x + d) % 4, 1024)], target.at[x], p.along_x(d))
            )
    for d, one in zip(STEPS, key_x):
        one.wait_recv()
        column = wk.at[:, (x + 4 - d) % 4, :, c]
        to_core.append(cp.start(column, column, p.sibling()))
    for d, one in zip(STEPS, value_y):
        one.wait_recv()
        from_u, from_w = p.y_at(4 - d)
        row = wv.at[from_u, :, from_w, c]
        to_core.append(cp.start(row, row, p.sibling()))
    for one in own_hidden:
        one.wait()
    for one in to_core:
        one.wait_recv()
    later += [move(wk, wk_out), move(wv, wv_out), move(hid.at[z], hid_out.at[z])]

    def project(slot, weights):
        return jnp.dot(hid[slot], weights[...].reshape(2048, 512), preferred_element_type=F32)

    k_own[...] = project(z, wk)
    v_own[...] = project(z, wv)
    back = []
    for number, d in enumerate(STEPS):
        slot = (z + 4 - d) % 4
        whole[number].wait_recv()
        later.append(move(hid.at[slot], hid_out.at[slot]))
        k_part[number] = project(slot, wk)
        back.append(cp.start(k_part.at[number], k_in.at[number], p.along_z(4 - d)))
        v_part[number] = project(slot, wv).astype(BF)
        back.append(cp.start(v_part.at[number], v_in.at[number], p.along_z(4 - d)))
    for one in back:
        one.wait_recv()
    cos, sin = cosine[...], sine[...]
    for h in range(KV_HEADS):
        part = slice(h * HD, (h + 1) * HD)
        k, v = k_own[:, part], v_own[:, part]
        for number in range(3):
            k = k + k_in[number, :, part]
            v = v + v_in[number, :, part].astype(F32)
        kv[:, 2 * h * HD : (2 * h + 1) * HD] = (k * cos + turn(k) * sin).astype(BF)
        kv[:, (2 * h + 1) * HD : (2 * h + 2) * HD] = v.astype(BF)
    later.append(move(kv.at[:, lanes(x, 256)], kv_h.at[u, x]))
    sent += [
        cp.start(kv.at[:, lanes((x + dx) % 4, 256)], kv_h.at[u, x], p.in_group(du, dx))
        for du, dx in GROUP
    ]
    for one in sent:
        one.wait_recv()
    for one in key_y + value_x + whole + key_x + value_y + to_core + back + sent:
        one.wait_send()
    for one in later:
        one.wait()


def forward(hidden, query, grad, wkey, wvalue, cosine, sine):
    shape = jax.ShapeDtypeStruct
    weights = (2, 4, 2, 2, 64, 512)
    return comm_call(
        forward_kernel,
        0,
        (
            shape((4, TOK, 2048), BF),
            shape(weights, BF),
            shape(weights, BF),
            shape((4, TOK, 1024), BF),
            shape((4, TOK, 1024), BF),
            shape((2, 4, TOK, 256), BF),
        ),
        [ANY] * 5 + [VMEM] * 2,
        (ANY,) * 6,
        42,
        19,
        (
            pltpu.VMEM((4, TOK, 2048), BF),
            pltpu.VMEM(weights, BF),
            pltpu.VMEM(weights, BF),
            pltpu.VMEM((3, TOK, 512), F32),
            pltpu.VMEM((3, TOK, 512), BF),
            pltpu.VMEM((3, TOK, 512), F32),
            pltpu.VMEM((3, TOK, 512), BF),
            pltpu.VMEM((TOK, 512), F32),
            pltpu.VMEM((TOK, 512), F32),
            pltpu.VMEM((TOK, 1024), BF),
        ),
    )(hidden, query, grad, wkey, wvalue, cosine, sine)


ROWS = 256


def attend_kernel(scalars, q, go, kv, dq, dkv, bias, kt, dk_sum, dv_sum):
    u = scalars[0]
    first, second = scalars[1], scalars[1] + scalars[2]
    scale = HD**-0.5
    contract = (((1,), (1,)), ((), ()))
    dk_sum[...] = jnp.zeros_like(dk_sum)
    dv_sum[...] = jnp.zeros_like(dv_sum)
    kt[...] = kv[:, :HD].astype(F32).T.astype(BF)

    def work(block, keys):
        at = slice(block * ROWS, (block + 1) * ROWS)
        key_at = lax.broadcasted_iota(jnp.int32, (keys, ROWS), 0)
        query_at = keys - ROWS + lax.broadcasted_iota(jnp.int32, (1, ROWS), 1)
        begin = jnp.where(query_at >= second, second, jnp.where(query_at >= first, first, 0))
        allowed = (key_at <= query_at) & (key_at >= begin)
        bias[:keys] = jnp.where(allowed, 0.0, NEGATIVE)

        def one_head(head, carry):
            query, grad = q[at, lanes(head, HD)], go[at, lanes(head, HD)]
            key, value = kv[:keys, :HD], kv[:keys, HD:]
            s = lax.dot_general(key, query, contract, preferred_element_type=F32) + bias[:keys]
            top = jnp.max(s, axis=0, keepdims=True)
            e = jnp.exp2((s - top) * (scale * LOG2E))
            weights = e * (1.0 / jnp.sum(e, axis=0, keepdims=True))
            low = weights.astype(BF)
            dw = lax.dot_general(value, grad, contract, preferred_element_type=F32)
            delta = jnp.sum(low.astype(F32) * dw, axis=0, keepdims=True)
            ds = (weights * (dw - delta)).astype(BF)
            dv_sum[:keys] += jnp.dot(low, grad, preferred_element_type=F32)
            dk_sum[:keys] += jnp.dot(ds, query, preferred_element_type=F32)
            turned = jnp.dot(kt[:, :keys], ds, preferred_element_type=F32)
            dq[at, lanes(head, HD)] = (turned.T * scale).astype(BF)
            return carry

        lax.fori_loop(0, 8, one_head, 0)

    for half in range(2):
        for block in range(2):
            pl.when(u == half)(functools.partial(work, block, (half * 2 + block + 1) * ROWS))
    dkv[:, :HD] = (dk_sum[...] * scale).astype(BF)
    dkv[:, HD:] = dv_sum[...].astype(BF)


def attend(scalars, q_h, go_h, kv_h):
    shape = jax.ShapeDtypeStruct
    return pl.pallas_call(
        attend_kernel,
        in_specs=[pl.BlockSpec(memory_space=pltpu.SMEM), VMEM, VMEM, VMEM],
        out_specs=[VMEM, VMEM],
        scratch_shapes=[
            pltpu.VMEM((1024, ROWS), F32),
            pltpu.VMEM((HD, 1024), BF),
            pltpu.VMEM((1024, HD), F32),
            pltpu.VMEM((1024, HD), F32),
        ],
        out_shape=[shape((512, 1024), BF), shape((1024, 256), BF)],
        compiler_params=pltpu.CompilerParams(vmem_limit_bytes=56 << 20),
    )(scalars, q_h, go_h, kv_h)


def backward_kernel(
    dkv, dq_h, hid_in, wk_in, wv_in, cosine, sine,
    dq, dhidden, grad_key, grad_value,
    send, recv, here, came, rows, hid, turned, wk, wv, dh, mine, low, away, other, terms,
):
    p = Peers()
    u, x, z, w, c = p.u, p.x, p.z, p.w, p.c
    cp = Copies(send, recv)
    used = [0]

    def move(src, dst):
        copy = pltpu.make_async_copy(src, dst, here.at[used[0]])
        used[0] += 1
        copy.start()
        return copy

    hid_load = move(hid_in, hid)
    first = move(dkv.at[u, x], came.at[u, x])
    weight_loads = [move(wk_in, wk), move(wv_in, wv)]
    later = [move(dq_h.at[x], dq.at[:, lanes(x, 1024)])]
    meet(
        [p.along_z(d) for d in STEPS]
        + [p.on_plane(dy, dx) for dy, dx in PLANE]
        + [p.sibling()]
    )
    pieces = [
        cp.start(dkv.at[(u + du) % 2, (x + dx) % 4], came.at[u, x], p.in_group(du, dx))
        for du, dx in GROUP
    ]
    hid_load.wait()

    def transpose(k, carry):
        block = hid[:, :, lanes(k, 128)].reshape(512, 128)
        turned[k] = block.astype(F32).T.astype(BF)
        return carry

    lax.fori_loop(0, 16, transpose, 0)
    first.wait()
    for one in pieces:
        one.wait_recv()
    cos, sin = cosine[...], sine[...]
    for h in range(KV_HEADS):
        total = came[0, h].astype(F32) + came[1, h].astype(F32)
        dk = total[:, :HD]
        rows[z, :, h * HD : (h + 1) * HD] = (dk * cos - turn(dk) * sin).astype(BF)
        rows[z, :, 512 + h * HD : 512 + (h + 1) * HD] = total[:, HD:].astype(BF)
    sent_z = [cp.start(rows.at[z], rows.at[z], p.along_z(d)) for d in STEPS]
    sent = [
        cp.start(dq_h.at[(x + d) % 4], dq.at[:, lanes(x, 1024)], p.along_x(d)) for d in STEPS
    ]
    for one in weight_loads:
        one.wait()
    contract = (((1,), (1,)), ((), ()))

    def hidden_rows(slot, number):
        def one(piece, carry):
            key = wk[piece // 4, piece % 4].reshape(256, 512)
            value = wv[piece // 4, piece % 4].reshape(256, 512)
            total = lax.dot_general(
                rows[slot, :, :512], key, contract, preferred_element_type=F32
            ) + lax.dot_general(rows[slot, :, 512:], value, contract, preferred_element_type=F32)
            dh[number, :, lanes(piece, 256)] = total.astype(BF)
            return carry

        lax.fori_loop(0, 8, one, 0)

    hidden_rows(z, 3)
    for piece in range(8):
        later.append(
            move(
                dh.at[3, :, pl.ds(piece * 256, 256)],
                dhidden.at[:, lanes(piece * 4 + z, 256)],
            )
        )
    whole = []
    for number, d in enumerate(STEPS):
        slot = (z + 4 - d) % 4
        sent_z[number].wait_recv()
        hidden_rows(slot, number)
        at = cp.used
        for piece in range(8):
            cp.used = at
            cp.start(
                dh.at[number, :, pl.ds(piece * 256, 256)],
                dhidden.at[:, lanes(piece * 4 + z, 256)],
                p.along_z(4 - d),
            )
        cp.used = at
        whole.append(cp.make(dh.at[number], dh.at[number], p.along_z(4 - d)))
    order = PLANE + [(0, 0)]
    swapped, out = [], []

    def pass_on(k):
        swapped[k].wait_recv()
        low[k] = (mine[k] + other[k].astype(F32)).astype(BF)
        dy, dx = order[k]
        if k < 15:
            out.append(cp.start(low.at[k], terms.at[k], p.on_plane(dy, dx)))

    for k, (dy, dx) in enumerate(order):
        tu, tw = p.y_at(dy)
        block = (tu * 4 + (x + dx) % 4) * 2 + tw
        product = jnp.dot(
            turned[block], rows[...].reshape(512, 1024), preferred_element_type=F32
        )
        zero_core = c == 0
        mine[k] = jnp.where(zero_core, product[:64], product[64:])
        away[k] = jnp.where(zero_core, product[64:], product[:64]).astype(BF)
        swapped.append(cp.start(away.at[k], other.at[k], p.sibling()))
        if k >= 2:
            pass_on(k - 2)
    pass_on(14)
    pass_on(15)
    for one in out:
        one.wait_recv()
    total = low[15].astype(F32)
    for k in range(15):
        total = total + terms[k].astype(F32)
    grad_key[...] = total[:, :512]
    grad_value[...] = total[:, 512:]
    for one in whole + sent:
        one.wait_recv()
    for one in pieces + sent_z + sent + whole + swapped + out:
        one.wait_send()
    for one in later:
        one.wait()


def backward(dkv, dq_h, hid_g, wk, wv, cosine, sine):
    shape = jax.ShapeDtypeStruct
    weights = (2, 4, 2, 2, 64, 512)
    return comm_call(
        backward_kernel,
        1,
        (
            shape((TOK, 4096), BF),
            shape((TOK, WIDE), BF),
            shape((64, 512), F32),
            shape((64, 512), F32),
        ),
        [ANY] * 5 + [VMEM] * 2,
        (ANY, ANY, VMEM, VMEM),
        7 + 3 + 3 + 3 + 16 + 15,
        13,
        (
            pltpu.VMEM((2, 4, TOK, 256), BF),
            pltpu.VMEM((4, TOK, 1024), BF),
            pltpu.VMEM((4, TOK, 2048), BF),
            pltpu.VMEM((16, TOK, 512), BF),
            pltpu.VMEM(weights, BF),
            pltpu.VMEM(weights, BF),
            pltpu.VMEM((4, TOK, 2048), BF),
            pltpu.VMEM((16, 64, 1024), F32),
            pltpu.VMEM((16, 64, 1024), BF),
            pltpu.VMEM((16, 64, 1024), BF),
            pltpu.VMEM((16, 64, 1024), BF),
            pltpu.VMEM((15, 64, 1024), BF),
        ),
    )(dkv, dq_h, hid_g, wk, wv, cosine, sine)


def local(hidden, queries, grad_out, key_weight, value_weight, doc_lengths):
    lengths = doc_lengths[0]
    zero = lax.axis_index("zero")
    cosine, sine = own_tables(lengths, zero * TOK)
    hid_g, wk, wv, q_h, go_h, kv_h = forward(
        hidden[0], queries[0], grad_out[0], key_weight, value_weight, cosine, sine
    )
    scalars = jnp.concatenate([(zero // 4).astype(jnp.int32)[None], lengths])
    dq_h, dkv = attend(
        scalars, q_h.reshape(512, 1024), go_h.reshape(512, 1024), kv_h.reshape(1024, 256)
    )
    dquery, dhidden, grad_key, grad_value = backward(
        dkv.reshape(2, 4, TOK, 256), dq_h.reshape(4, TOK, 1024), hid_g, wk, wv, cosine, sine
    )
    return dquery[None], dhidden[None], grad_key, grad_value


def solution(mesh):
    return jax.shard_map(
        local,
        mesh=mesh,
        in_specs=(
            P("dp", "zero", None),
            P("dp", "zero", None),
            P("dp", "zero", None),
            P(("zero", "dp"), None),
            P(("zero", "dp"), None),
            P("dp", None),
        ),
        out_specs=(
            P("dp", "zero", None),
            P("dp", "zero", None),
            P(("zero", "dp"), None),
            P(("zero", "dp"), None),
        ),
        check_vma=False,
    )
```

```python
import functools

import jax
import jax.numpy as jnp
from jax import lax
from jax.experimental import pallas as pl
from jax.experimental.pallas import tpu as pltpu
from jax.sharding import PartitionSpec as P

KV_HEADS = 4
HD = 128
ROPE_BASE = 500000.0
NEGATIVE = -1e30
LOG2E = 1.4426950408889634
MESH = pl.DeviceIdType.MESH
TOK = 128
WIDE = 8192
ANY = pl.BlockSpec(memory_space=pl.ANY)
VMEM = pl.BlockSpec(memory_space=pltpu.VMEM)
BF = jnp.bfloat16
F32 = jnp.float32


def own_tables(lengths, offset):
    at = offset + lax.broadcasted_iota(jnp.int32, (TOK, HD), 0)
    first, second = lengths[0], lengths[0] + lengths[1]
    begin = jnp.where(at >= second, second, jnp.where(at >= first, first, 0))
    lane = lax.broadcasted_iota(jnp.int32, (TOK, HD), 1)
    frequency = ROPE_BASE ** (-2.0 * (lane % (HD // 2)).astype(F32) / HD)
    angles = (at - begin).astype(F32) * frequency
    return jnp.cos(angles), jnp.where(lane < HD // 2, -1.0, 1.0) * jnp.sin(angles)


def place():
    j, i = lax.axis_index("zero"), lax.axis_index("dp")
    return j // 4, j % 4, i // 4, (i // 2) % 2, i % 2


def device(u, x, z, w, c):
    return (u * 4 + x, z * 4 + w * 2 + c)


class Peers:
    def __init__(self):
        self.u, self.x, self.z, self.w, self.c = place()

    def along_x(self, d):
        return device(self.u, (self.x + d) % 4, self.z, self.w, self.c)

    def along_z(self, d):
        return device(self.u, self.x, (self.z + d) % 4, self.w, self.c)

    def y_at(self, d):
        y = (2 * self.u + self.w + d) % 4
        return y // 2, y % 2

    def along_y(self, d):
        u, w = self.y_at(d)
        return device(u, self.x, self.z, w, self.c)

    def in_group(self, du, dx):
        return device((self.u + du) % 2, (self.x + dx) % 4, self.z, self.w, self.c)

    def on_plane(self, dy, dx):
        u, w = self.y_at(dy)
        return device(u, (self.x + dx) % 4, self.z, w, self.c)

    def sibling(self):
        return device(self.u, self.x, self.z, self.w, 1 - self.c)


def meet(devices):
    barrier = pltpu.get_barrier_semaphore()
    for one in devices:
        pl.semaphore_signal(barrier, inc=1, device_id=one, device_id_type=MESH)
    pl.semaphore_wait(barrier, len(devices))


class Copies:
    def __init__(self, send, recv):
        self.send, self.recv, self.used = send, recv, 0

    def make(self, src, dst, to):
        at = self.used
        self.used += 1
        return pltpu.make_async_remote_copy(
            src_ref=src,
            dst_ref=dst,
            send_sem=self.send.at[at],
            recv_sem=self.recv.at[at],
            device_id=to,
            device_id_type=MESH,
        )

    def start(self, src, dst, to):
        copy = self.make(src, dst, to)
        copy.start()
        return copy


GROUP = [(du, dx) for du in (1, 0) for dx in (2, 1, 3, 0)][:-1]
PLANE = [(dy, dx) for dy in (2, 1, 3, 0) for dx in (2, 1, 3, 0)][:-1]
STEPS = (1, 3, 2)


def comm_call(kernel, number, outs, in_specs, out_specs, remote, local, scratch=()):
    return pl.pallas_call(
        kernel,
        out_shape=outs,
        in_specs=in_specs,
        out_specs=out_specs,
        scratch_shapes=[
            pltpu.SemaphoreType.DMA((remote,)),
            pltpu.SemaphoreType.DMA((remote,)),
            pltpu.SemaphoreType.DMA((local,)),
            *scratch,
        ],
        compiler_params=pltpu.CompilerParams(
            collective_id=number, has_side_effects=True, vmem_limit_bytes=60 << 20
        ),
    )


def lanes(at, size):
    return pl.ds(pl.multiple_of(at * size, size), size)


def turn(rows):
    return pltpu.roll(rows, HD // 2, 1)


def forward_kernel(
    hidden, query, grad, wkey, wvalue, cosine, sine,
    hid_out, wk_out, wv_out, q_h, go_h, kv_h,
    send, recv, here, hid, wk, wv, k_part, v_part, k_in, v_in, k_own, v_own, kv,
):
    p = Peers()
    u, x, z, w, c = p.u, p.x, p.z, p.w, p.c
    cp = Copies(send, recv)
    used = [0]

    def move(src, dst):
        copy = pltpu.make_async_copy(src, dst, here.at[used[0]])
        used[0] += 1
        copy.start()
        return copy

    own_key = move(wkey, wk.at[u, x, w, c])
    own_value = move(wvalue, wv.at[u, x, w, c])
    own_hidden = [
        move(hidden.at[:, lanes(piece * 4 + z, 256)], hid.at[z, :, pl.ds(piece * 256, 256)])
        for piece in range(8)
    ]
    later = [
        move(query.at[:, lanes(x, 1024)], q_h.at[x]),
        move(grad.at[:, lanes(x, 1024)], go_h.at[x]),
    ]
    meet(
        [p.along_z(d) for d in STEPS]
        + [p.on_plane(dy, 0) for dy in STEPS]
        + [p.on_plane(0, dx) for dx in STEPS]
        + [p.on_plane(2, dx) for dx in STEPS]
        + [p.sibling()]
    )
    key_y = [cp.start(wkey, wk.at[u, x, w, c], p.along_y(d)) for d in STEPS]
    value_x = [cp.start(wvalue, wv.at[u, x, w, c], p.along_x(d)) for d in STEPS]
    whole = []
    for d in STEPS:
        there, at = (z + d) % 4, cp.used
        for piece in range(8):
            cp.used = at
            cp.start(
                hidden.at[:, lanes(piece * 4 + there, 256)],
                hid.at[z, :, pl.ds(piece * 256, 256)],
                p.along_z(d),
            )
        cp.used = at
        came = (z + 4 - d) % 4
        whole.append(cp.make(hid.at[came], hid.at[came], p.along_z(d)))
    own_key.wait()
    for one in key_y:
        one.wait_recv()
    column = wk.at[:, x, :, c]
    key_x = [cp.start(column, column, p.along_x(d)) for d in STEPS]
    to_core = [cp.start(column, column, p.sibling())]
    own_value.wait()
    for one in value_x:
        one.wait_recv()
    row = wv.at[u, :, w, c]
    value_y = [cp.start(row, row, p.along_y(d)) for d in STEPS]
    to_core.append(cp.start(row, row, p.sibling()))
    sent = []
    for source, target in ((query, q_h), (grad, go_h)):
        for d in STEPS:
            sent.append(
                cp.start(source.at[:, lanes((x + d) % 4, 1024)], target.at[x], p.along_x(d))
            )
    for d, one in zip(STEPS, key_x):
        one.wait_recv()
        column = wk.at[:, (x + 4 - d) % 4, :, c]
        to_core.append(cp.start(column, column, p.sibling()))
    for d, one in zip(STEPS, value_y):
        one.wait_recv()
        from_u, from_w = p.y_at(4 - d)
        row = wv.at[from_u, :, from_w, c]
        to_core.append(cp.start(row, row, p.sibling()))
    for one in own_hidden:
        one.wait()
    for one in to_core:
        one.wait_recv()
    later += [move(wk, wk_out), move(wv, wv_out), move(hid.at[z], hid_out.at[z])]

    def project(slot, weights):
        return jnp.dot(hid[slot], weights[...].reshape(2048, 512), preferred_element_type=F32)

    k_own[...] = project(z, wk)
    v_own[...] = project(z, wv)
    back = []
    for number, d in enumerate(STEPS):
        slot = (z + 4 - d) % 4
        whole[number].wait_recv()
        later.append(move(hid.at[slot], hid_out.at[slot]))
        k_part[number] = project(slot, wk)
        back.append(cp.start(k_part.at[number], k_in.at[number], p.along_z(4 - d)))
        v_part[number] = project(slot, wv).astype(BF)
        back.append(cp.start(v_part.at[number], v_in.at[number], p.along_z(4 - d)))
    for one in back:
        one.wait_recv()
    cos, sin = cosine[...], sine[...]
    for h in range(KV_HEADS):
        part = slice(h * HD, (h + 1) * HD)
        k, v = k_own[:, part], v_own[:, part]
        for number in range(3):
            k = k + k_in[number, :, part]
            v = v + v_in[number, :, part].astype(F32)
        kv[:, 2 * h * HD : (2 * h + 1) * HD] = (k * cos + turn(k) * sin).astype(BF)
        kv[:, (2 * h + 1) * HD : (2 * h + 2) * HD] = v.astype(BF)
    later.append(move(kv.at[:, lanes(x, 256)], kv_h.at[u, x]))
    across = [
        cp.make(kv.at[:, lanes((x + dx) % 4, 256)], kv_h.at[u, x], p.in_group(1, dx))
        for dx in (2, 1, 3, 0)
    ]

    @pl.when(u == 0)
    def _():
        for one in across:
            one.start()

    sent += [
        cp.start(kv.at[:, lanes((x + dx) % 4, 256)], kv_h.at[u, x], p.along_x(dx))
        for dx in STEPS
    ]
    for one in sent:
        one.wait_recv()

    @pl.when(u == 0)
    def _():
        for one in across:
            one.wait_send()

    @pl.when(u == 1)
    def _():
        for one in across:
            one.wait_recv()

    for one in key_y + value_x + whole + key_x + value_y + to_core + back + sent:
        one.wait_send()
    for one in later:
        one.wait()


def forward(hidden, query, grad, wkey, wvalue, cosine, sine):
    shape = jax.ShapeDtypeStruct
    weights = (2, 4, 2, 2, 64, 512)
    return comm_call(
        forward_kernel,
        0,
        (
            shape((4, TOK, 2048), BF),
            shape(weights, BF),
            shape(weights, BF),
            shape((4, TOK, 1024), BF),
            shape((4, TOK, 1024), BF),
            shape((2, 4, TOK, 256), BF),
        ),
        [ANY] * 5 + [VMEM] * 2,
        (ANY,) * 6,
        42,
        19,
        (
            pltpu.VMEM((4, TOK, 2048), BF),
            pltpu.VMEM(weights, BF),
            pltpu.VMEM(weights, BF),
            pltpu.VMEM((3, TOK, 512), F32),
            pltpu.VMEM((3, TOK, 512), BF),
            pltpu.VMEM((3, TOK, 512), F32),
            pltpu.VMEM((3, TOK, 512), BF),
            pltpu.VMEM((TOK, 512), F32),
            pltpu.VMEM((TOK, 512), F32),
            pltpu.VMEM((TOK, 1024), BF),
        ),
    )(hidden, query, grad, wkey, wvalue, cosine, sine)


ROWS = 256


def attend_kernel(scalars, q, go, kv, dq, dkv, bias, kt, dk_sum, dv_sum):
    u = scalars[0]
    first, second = scalars[1], scalars[1] + scalars[2]
    scale = HD**-0.5
    contract = (((1,), (1,)), ((), ()))
    dk_sum[...] = jnp.zeros_like(dk_sum)
    dv_sum[...] = jnp.zeros_like(dv_sum)
    kt[...] = kv[:, :HD].astype(F32).T.astype(BF)

    def work(block, keys):
        at = slice(block * ROWS, (block + 1) * ROWS)
        key_at = lax.broadcasted_iota(jnp.int32, (keys, ROWS), 0)
        query_at = keys - ROWS + lax.broadcasted_iota(jnp.int32, (1, ROWS), 1)
        begin = jnp.where(query_at >= second, second, jnp.where(query_at >= first, first, 0))
        allowed = (key_at <= query_at) & (key_at >= begin)
        bias[:keys] = jnp.where(allowed, 0.0, NEGATIVE)

        def one_head(head, carry):
            query, grad = q[at, lanes(head, HD)], go[at, lanes(head, HD)]
            key, value = kv[:keys, :HD], kv[:keys, HD:]
            s = lax.dot_general(key, query, contract, preferred_element_type=F32) + bias[:keys]
            top = jnp.max(s, axis=0, keepdims=True)
            e = jnp.exp2((s - top) * (scale * LOG2E))
            weights = e * (1.0 / jnp.sum(e, axis=0, keepdims=True))
            low = weights.astype(BF)
            dw = lax.dot_general(value, grad, contract, preferred_element_type=F32)
            delta = jnp.sum(low.astype(F32) * dw, axis=0, keepdims=True)
            ds = (weights * (dw - delta)).astype(BF)
            dv_sum[:keys] += jnp.dot(low, grad, preferred_element_type=F32)
            dk_sum[:keys] += jnp.dot(ds, query, preferred_element_type=F32)
            turned = jnp.dot(kt[:, :keys], ds, preferred_element_type=F32)
            dq[at, lanes(head, HD)] = (turned.T * scale).astype(BF)
            return carry

        lax.fori_loop(0, 8, one_head, 0)

    for half in range(2):
        for block in range(2):
            pl.when(u == half)(functools.partial(work, block, (half * 2 + block + 1) * ROWS))
    dkv[:, :HD] = (dk_sum[...] * scale).astype(BF)
    dkv[:, HD:] = dv_sum[...].astype(BF)


def attend(scalars, q_h, go_h, kv_h):
    shape = jax.ShapeDtypeStruct
    return pl.pallas_call(
        attend_kernel,
        in_specs=[pl.BlockSpec(memory_space=pltpu.SMEM), VMEM, VMEM, VMEM],
        out_specs=[VMEM, VMEM],
        scratch_shapes=[
            pltpu.VMEM((1024, ROWS), F32),
            pltpu.VMEM((HD, 1024), BF),
            pltpu.VMEM((1024, HD), F32),
            pltpu.VMEM((1024, HD), F32),
        ],
        out_shape=[shape((512, 1024), BF), shape((1024, 256), BF)],
        compiler_params=pltpu.CompilerParams(vmem_limit_bytes=56 << 20),
    )(scalars, q_h, go_h, kv_h)


def backward_kernel(
    dkv, dq_h, hid_in, wk_in, wv_in, cosine, sine,
    dq, dhidden, grad_key, grad_value,
    send, recv, here, came, rows, hid, turned, wk, wv, dh, mine, low, away, other,
    key_in, value_in, key_sum, value_sum, key_last, value_last,
):
    p = Peers()
    u, x, z, w, c = p.u, p.x, p.z, p.w, p.c
    cp = Copies(send, recv)
    used = [0]

    def move(src, dst):
        copy = pltpu.make_async_copy(src, dst, here.at[used[0]])
        used[0] += 1
        copy.start()
        return copy

    hid_load = move(hid_in, hid)
    first = move(dkv.at[u, x], came.at[u, x])
    weight_loads = [move(wk_in, wk), move(wv_in, wv)]
    later = [move(dq_h.at[x], dq.at[:, lanes(x, 1024)])]
    meet(
        [p.along_z(d) for d in STEPS]
        + [p.on_plane(dy, dx) for dy, dx in PLANE]
        + [p.sibling()]
    )
    across = [
        cp.make(dkv.at[0, (x + dx) % 4], came.at[1, x], p.in_group(1, dx))
        for dx in (2, 1, 3, 0)
    ]

    @pl.when(u == 1)
    def _():
        for one in across:
            one.start()
        came[0] = jnp.zeros((4, TOK, 256), BF)

    pieces = [
        cp.start(dkv.at[u, (x + dx) % 4], came.at[u, x], p.along_x(dx)) for dx in STEPS
    ]
    hid_load.wait()

    def transpose(k, carry):
        block = hid[:, :, lanes(k, 128)].reshape(512, 128)
        turned[k] = block.astype(F32).T.astype(BF)
        return carry

    lax.fori_loop(0, 16, transpose, 0)
    first.wait()
    for one in pieces:
        one.wait_recv()

    @pl.when(u == 0)
    def _():
        for one in across:
            one.wait_recv()

    @pl.when(u == 1)
    def _():
        for one in across:
            one.wait_send()

    cos, sin = cosine[...], sine[...]
    for h in range(KV_HEADS):
        total = came[0, h].astype(F32) + came[1, h].astype(F32)
        dk = total[:, :HD]
        rows[z, :, h * HD : (h + 1) * HD] = (dk * cos - turn(dk) * sin).astype(BF)
        rows[z, :, 512 + h * HD : 512 + (h + 1) * HD] = total[:, HD:].astype(BF)
    sent_z = [cp.start(rows.at[z], rows.at[z], p.along_z(d)) for d in STEPS]
    sent = [
        cp.start(dq_h.at[(x + d) % 4], dq.at[:, lanes(x, 1024)], p.along_x(d)) for d in STEPS
    ]
    for one in weight_loads:
        one.wait()
    contract = (((1,), (1,)), ((), ()))

    def hidden_rows(slot, number):
        def one(piece, carry):
            key = wk[piece // 4, piece % 4].reshape(256, 512)
            value = wv[piece // 4, piece % 4].reshape(256, 512)
            total = lax.dot_general(
                rows[slot, :, :512], key, contract, preferred_element_type=F32
            ) + lax.dot_general(rows[slot, :, 512:], value, contract, preferred_element_type=F32)
            dh[number, :, lanes(piece, 256)] = total.astype(BF)
            return carry

        lax.fori_loop(0, 8, one, 0)

    hidden_rows(z, 3)
    for piece in range(8):
        later.append(
            move(
                dh.at[3, :, pl.ds(piece * 256, 256)],
                dhidden.at[:, lanes(piece * 4 + z, 256)],
            )
        )
    whole = []
    for number, d in enumerate(STEPS):
        slot = (z + 4 - d) % 4
        sent_z[number].wait_recv()
        hidden_rows(slot, number)
        at = cp.used
        for piece in range(8):
            cp.used = at
            cp.start(
                dh.at[number, :, pl.ds(piece * 256, 256)],
                dhidden.at[:, lanes(piece * 4 + z, 256)],
                p.along_z(4 - d),
            )
        cp.used = at
        whole.append(cp.make(dh.at[number], dh.at[number], p.along_z(4 - d)))
    order = PLANE + [(0, 0)]
    y = 2 * u + w
    swapped, key_out, value_out = [], {}, {}

    def pass_on(k):
        swapped[k].wait_recv()
        low[k] = (mine[k] + other[k].astype(F32)).astype(BF)
        dy, dx = order[k]
        if dx:
            key_out[dy, dx] = cp.start(
                low.at[k, :, pl.ds(0, 512)], key_in.at[dx - 1, (y + dy) % 4], p.along_x(dx)
            )
        if dy:
            value_out[dy, dx] = cp.start(
                low.at[k, :, pl.ds(512, 512)], value_in.at[dy - 1, (x + dx) % 4], p.along_y(dy)
            )

    for k, (dy, dx) in enumerate(order):
        tu, tw = p.y_at(dy)
        block = (tu * 4 + (x + dx) % 4) * 2 + tw
        product = jnp.dot(
            turned[block], rows[...].reshape(512, 1024), preferred_element_type=F32
        )
        zero_core = c == 0
        mine[k] = jnp.where(zero_core, product[:64], product[64:])
        away[k] = jnp.where(zero_core, product[64:], product[:64]).astype(BF)
        swapped.append(cp.start(away.at[k], other.at[k], p.sibling()))
        if k >= 2:
            pass_on(k - 2)
    pass_on(14)
    pass_on(15)
    last = []
    for d in (2, 1, 3, 0):
        for one in range(1, 4):
            key_out[d, one].wait_recv()
        at = order.index((d, 0))
        total = low[at, :, :512].astype(F32)
        for one in range(3):
            total = total + key_in[one, (y + d) % 4].astype(F32)
        if d:
            key_sum[d - 1] = total.astype(BF)
            last.append(cp.start(key_sum.at[d - 1], key_last.at[d - 1], p.along_y(d)))
        else:
            grad_key[...] = total
        for one in range(1, 4):
            value_out[one, d].wait_recv()
        at = order.index((0, d))
        total = low[at, :, 512:].astype(F32)
        for one in range(3):
            total = total + value_in[one, (x + d) % 4].astype(F32)
        if d:
            value_sum[d - 1] = total.astype(BF)
            last.append(cp.start(value_sum.at[d - 1], value_last.at[d - 1], p.along_x(d)))
        else:
            grad_value[...] = total
    for one in last:
        one.wait_recv()
    for one in range(3):
        grad_key[...] += key_last[one].astype(F32)
        grad_value[...] += value_last[one].astype(F32)
    out = list(key_out.values()) + list(value_out.values()) + last
    for one in whole + sent:
        one.wait_recv()
    for one in pieces + sent_z + sent + whole + swapped + out:
        one.wait_send()
    for one in later:
        one.wait()


def backward(dkv, dq_h, hid_g, wk, wv, cosine, sine):
    shape = jax.ShapeDtypeStruct
    weights = (2, 4, 2, 2, 64, 512)
    return comm_call(
        backward_kernel,
        1,
        (
            shape((TOK, 4096), BF),
            shape((TOK, WIDE), BF),
            shape((64, 512), F32),
            shape((64, 512), F32),
        ),
        [ANY] * 5 + [VMEM] * 2,
        (ANY, ANY, VMEM, VMEM),
        7 + 3 + 3 + 3 + 16 + 12 + 12 + 6,
        13,
        (
            pltpu.VMEM((2, 4, TOK, 256), BF),
            pltpu.VMEM((4, TOK, 1024), BF),
            pltpu.VMEM((4, TOK, 2048), BF),
            pltpu.VMEM((16, TOK, 512), BF),
            pltpu.VMEM(weights, BF),
            pltpu.VMEM(weights, BF),
            pltpu.VMEM((4, TOK, 2048), BF),
            pltpu.VMEM((16, 64, 1024), F32),
            pltpu.VMEM((16, 64, 1024), BF),
            pltpu.VMEM((16, 64, 1024), BF),
            pltpu.VMEM((16, 64, 1024), BF),
            pltpu.VMEM((3, 4, 64, 512), BF),
            pltpu.VMEM((3, 4, 64, 512), BF),
            *[pltpu.VMEM((3, 64, 512), BF)] * 4,
        ),
    )(dkv, dq_h, hid_g, wk, wv, cosine, sine)


def local(hidden, queries, grad_out, key_weight, value_weight, doc_lengths):
    lengths = doc_lengths[0]
    zero = lax.axis_index("zero")
    cosine, sine = own_tables(lengths, zero * TOK)
    hid_g, wk, wv, q_h, go_h, kv_h = forward(
        hidden[0], queries[0], grad_out[0], key_weight, value_weight, cosine, sine
    )
    scalars = jnp.concatenate([(zero // 4).astype(jnp.int32)[None], lengths])
    dq_h, dkv = attend(
        scalars, q_h.reshape(512, 1024), go_h.reshape(512, 1024), kv_h.reshape(1024, 256)
    )
    dquery, dhidden, grad_key, grad_value = backward(
        dkv.reshape(2, 4, TOK, 256), dq_h.reshape(4, TOK, 1024), hid_g, wk, wv, cosine, sine
    )
    return dquery[None], dhidden[None], grad_key, grad_value


def solution(mesh):
    return jax.shard_map(
        local,
        mesh=mesh,
        in_specs=(
            P("dp", "zero", None),
            P("dp", "zero", None),
            P("dp", "zero", None),
            P(("zero", "dp"), None),
            P(("zero", "dp"), None),
            P("dp", None),
        ),
        out_specs=(
            P("dp", "zero", None),
            P("dp", "zero", None),
            P(("zero", "dp"), None),
            P(("zero", "dp"), None),
        ),
        check_vma=False,
    )
```

```python
import functools

import jax
import jax.numpy as jnp
import numpy as np
from jax import lax
from jax.experimental import pallas as pl
from jax.experimental.pallas import tpu as pltpu
from jax.sharding import PartitionSpec as P

KV_HEADS = 4
HD = 128
ROPE_BASE = 500000.0
NEGATIVE = -1e30
LOG2E = 1.4426950408889634
MESH = pl.DeviceIdType.MESH
TOK = 128
WIDE = 8192
ANY = pl.BlockSpec(memory_space=pl.ANY)
VMEM = pl.BlockSpec(memory_space=pltpu.VMEM)
BF = jnp.bfloat16
F32 = jnp.float32


FREQUENCY = (ROPE_BASE ** (-2.0 * (np.arange(HD) % (HD // 2)) / HD)).astype(np.float32)


def begin_of(at, first, second):
    return jnp.where(at >= second, second, jnp.where(at >= first, first, 0))


def place():
    j, i = lax.axis_index("zero"), lax.axis_index("dp")
    return j // 4, j % 4, i // 4, (i // 2) % 2, i % 2


def device(u, x, z, w, c):
    return (u * 4 + x, z * 4 + w * 2 + c)


class Peers:
    def __init__(self):
        self.u, self.x, self.z, self.w, self.c = place()

    def along_x(self, d):
        return device(self.u, (self.x + d) % 4, self.z, self.w, self.c)

    def along_z(self, d):
        return device(self.u, self.x, (self.z + d) % 4, self.w, self.c)

    def y_at(self, d):
        y = (2 * self.u + self.w + d) % 4
        return y // 2, y % 2

    def along_y(self, d):
        u, w = self.y_at(d)
        return device(u, self.x, self.z, w, self.c)

    def in_group(self, du, dx):
        return device((self.u + du) % 2, (self.x + dx) % 4, self.z, self.w, self.c)

    def on_plane(self, dy, dx):
        u, w = self.y_at(dy)
        return device(u, (self.x + dx) % 4, self.z, w, self.c)

    def sibling(self):
        return device(self.u, self.x, self.z, self.w, 1 - self.c)


def meet(devices):
    barrier = pltpu.get_barrier_semaphore()
    for one in devices:
        pl.semaphore_signal(barrier, inc=1, device_id=one, device_id_type=MESH)
    pl.semaphore_wait(barrier, len(devices))


class Copies:
    def __init__(self, send, recv):
        self.send, self.recv, self.used = send, recv, 0

    def make(self, src, dst, to):
        at = self.used
        self.used += 1
        return pltpu.make_async_remote_copy(
            src_ref=src,
            dst_ref=dst,
            send_sem=self.send.at[at],
            recv_sem=self.recv.at[at],
            device_id=to,
            device_id_type=MESH,
        )

    def start(self, src, dst, to):
        copy = self.make(src, dst, to)
        copy.start()
        return copy


GROUP = [(du, dx) for du in (1, 0) for dx in (2, 1, 3, 0)][:-1]
PLANE = [(dy, dx) for dy in (2, 1, 3, 0) for dx in (2, 1, 3, 0)][:-1]
STEPS = (1, 3, 2)


def comm_call(kernel, number, outs, in_specs, out_specs, remote, local, scratch=()):
    return pl.pallas_call(
        kernel,
        out_shape=outs,
        in_specs=in_specs,
        out_specs=out_specs,
        scratch_shapes=[
            pltpu.SemaphoreType.DMA((remote,)),
            pltpu.SemaphoreType.DMA((remote,)),
            pltpu.SemaphoreType.DMA((local,)),
            *scratch,
        ],
        compiler_params=pltpu.CompilerParams(
            collective_id=number, has_side_effects=True, vmem_limit_bytes=60 << 20
        ),
    )


def lanes(at, size):
    return pl.ds(pl.multiple_of(at * size, size), size)


def turn(rows):
    return pltpu.roll(rows, HD // 2, 1)


def forward_kernel(
    hidden, query, grad, wkey, wvalue, frequency, lengths,
    hid_out, wk_out, wv_out, q_h, go_h, kv_h, cosine, sine,
    send, recv, here, hid, wk, wv, k_part, v_part, k_in, v_in, k_own, v_own, kv,
):
    p = Peers()
    u, x, z, w, c = p.u, p.x, p.z, p.w, p.c
    cp = Copies(send, recv)
    used = [0]

    def move(src, dst):
        copy = pltpu.make_async_copy(src, dst, here.at[used[0]])
        used[0] += 1
        copy.start()
        return copy

    own_key = move(wkey, wk.at[u, x, w, c])
    own_value = move(wvalue, wv.at[u, x, w, c])
    own_hidden = [
        move(hidden.at[:, lanes(piece * 4 + z, 256)], hid.at[z, :, pl.ds(piece * 256, 256)])
        for piece in range(8)
    ]
    later = [
        move(query.at[:, lanes(x, 1024)], q_h.at[x]),
        move(grad.at[:, lanes(x, 1024)], go_h.at[x]),
    ]
    meet(
        [p.along_z(d) for d in STEPS]
        + [p.on_plane(dy, 0) for dy in STEPS]
        + [p.on_plane(0, dx) for dx in STEPS]
        + [p.on_plane(2, dx) for dx in STEPS]
        + [p.sibling()]
    )
    key_y = [cp.start(wkey, wk.at[u, x, w, c], p.along_y(d)) for d in STEPS]
    value_x = [cp.start(wvalue, wv.at[u, x, w, c], p.along_x(d)) for d in STEPS]
    whole = []
    for d in STEPS:
        there, at = (z + d) % 4, cp.used
        for piece in range(8):
            cp.used = at
            cp.start(
                hidden.at[:, lanes(piece * 4 + there, 256)],
                hid.at[z, :, pl.ds(piece * 256, 256)],
                p.along_z(d),
            )
        cp.used = at
        came = (z + 4 - d) % 4
        whole.append(cp.make(hid.at[came], hid.at[came], p.along_z(d)))
    at = (u * 4 + x) * TOK + lax.broadcasted_iota(jnp.int32, (TOK, HD), 0)
    begin = begin_of(at, lengths[0, 0], lengths[0, 0] + lengths[0, 1])
    angles = (at - begin).astype(F32) * frequency[...]
    sign = jnp.where(lax.broadcasted_iota(jnp.int32, (TOK, HD), 1) < HD // 2, -1.0, 1.0)
    cosine[...] = jnp.cos(angles)
    sine[...] = sign * jnp.sin(angles)
    own_key.wait()
    for one in key_y:
        one.wait_recv()
    column = wk.at[:, x, :, c]
    key_x = [cp.start(column, column, p.along_x(d)) for d in STEPS]
    to_core = [cp.start(column, column, p.sibling())]
    own_value.wait()
    for one in value_x:
        one.wait_recv()
    row = wv.at[u, :, w, c]
    value_y = [cp.start(row, row, p.along_y(d)) for d in STEPS]
    to_core.append(cp.start(row, row, p.sibling()))
    sent = []
    for source, target in ((query, q_h), (grad, go_h)):
        for d in STEPS:
            sent.append(
                cp.start(source.at[:, lanes((x + d) % 4, 1024)], target.at[x], p.along_x(d))
            )
    for d, one in zip(STEPS, key_x):
        one.wait_recv()
        column = wk.at[:, (x + 4 - d) % 4, :, c]
        to_core.append(cp.start(column, column, p.sibling()))
    for d, one in zip(STEPS, value_y):
        one.wait_recv()
        from_u, from_w = p.y_at(4 - d)
        row = wv.at[from_u, :, from_w, c]
        to_core.append(cp.start(row, row, p.sibling()))
    for one in own_hidden:
        one.wait()
    for one in to_core:
        one.wait_recv()
    later += [move(wk, wk_out), move(wv, wv_out), move(hid.at[z], hid_out.at[z])]

    def project(slot, weights):
        return jnp.dot(hid[slot], weights[...].reshape(2048, 512), preferred_element_type=F32)

    k_own[...] = project(z, wk)
    v_own[...] = project(z, wv)
    back = []
    for number, d in enumerate(STEPS):
        slot = (z + 4 - d) % 4
        whole[number].wait_recv()
        later.append(move(hid.at[slot], hid_out.at[slot]))
        k_part[number] = project(slot, wk)
        back.append(cp.start(k_part.at[number], k_in.at[number], p.along_z(4 - d)))
        v_part[number] = project(slot, wv).astype(BF)
        back.append(cp.start(v_part.at[number], v_in.at[number], p.along_z(4 - d)))
    for one in back:
        one.wait_recv()
    cos, sin = cosine[...], sine[...]
    for h in range(KV_HEADS):
        part = slice(h * HD, (h + 1) * HD)
        k, v = k_own[:, part], v_own[:, part]
        for number in range(3):
            k = k + k_in[number, :, part]
            v = v + v_in[number, :, part].astype(F32)
        kv[:, 2 * h * HD : (2 * h + 1) * HD] = (k * cos + turn(k) * sin).astype(BF)
        kv[:, (2 * h + 1) * HD : (2 * h + 2) * HD] = v.astype(BF)
    later.append(move(kv.at[:, lanes(x, 256)], kv_h.at[u, x]))
    across = [
        cp.make(kv.at[:, lanes((x + dx) % 4, 256)], kv_h.at[u, x], p.in_group(1, dx))
        for dx in (2, 1, 3, 0)
    ]

    @pl.when(u == 0)
    def _():
        for one in across:
            one.start()

    sent += [
        cp.start(kv.at[:, lanes((x + dx) % 4, 256)], kv_h.at[u, x], p.along_x(dx))
        for dx in STEPS
    ]
    for one in sent:
        one.wait_recv()

    @pl.when(u == 0)
    def _():
        for one in across:
            one.wait_send()

    @pl.when(u == 1)
    def _():
        for one in across:
            one.wait_recv()

    for one in key_y + value_x + whole + key_x + value_y + to_core + back + sent:
        one.wait_send()
    for one in later:
        one.wait()


def forward(hidden, query, grad, wkey, wvalue, lengths):
    shape = jax.ShapeDtypeStruct
    weights = (2, 4, 2, 2, 64, 512)
    return comm_call(
        forward_kernel,
        0,
        (
            shape((4, TOK, 2048), BF),
            shape(weights, BF),
            shape(weights, BF),
            shape((4, TOK, 1024), BF),
            shape((4, TOK, 1024), BF),
            shape((2, 4, TOK, 256), BF),
            shape((TOK, HD), F32),
            shape((TOK, HD), F32),
        ),
        [ANY] * 5 + [VMEM, pl.BlockSpec(memory_space=pltpu.SMEM)],
        (ANY,) * 6 + (VMEM,) * 2,
        42,
        19,
        (
            pltpu.VMEM((4, TOK, 2048), BF),
            pltpu.VMEM(weights, BF),
            pltpu.VMEM(weights, BF),
            pltpu.VMEM((3, TOK, 512), F32),
            pltpu.VMEM((3, TOK, 512), BF),
            pltpu.VMEM((3, TOK, 512), F32),
            pltpu.VMEM((3, TOK, 512), BF),
            pltpu.VMEM((TOK, 512), F32),
            pltpu.VMEM((TOK, 512), F32),
            pltpu.VMEM((TOK, 1024), BF),
        ),
    )(hidden, query, grad, wkey, wvalue, jnp.asarray(FREQUENCY)[None], lengths)


ROWS = 128
HEADS = 8


def attend_kernel(lengths, q, go, kv, dq, dkv, bias, kt, vt, dk_sum, dv_sum):
    u = lax.axis_index("zero") // 4
    first, second = lengths[0, 0], lengths[0, 0] + lengths[0, 1]
    scale = HD**-0.5
    contract = (((1,), (1,)), ((), ()))
    dk_sum[...] = jnp.zeros_like(dk_sum)
    dv_sum[...] = jnp.zeros_like(dv_sum)
    kt[...] = kv[:, :HD].astype(F32).T.astype(BF)
    vt[...] = kv[:, HD:].astype(F32).T.astype(BF)

    def work(block, keys):
        at = slice(block * ROWS, (block + 1) * ROWS)
        key_at = lax.broadcasted_iota(jnp.int32, (keys, ROWS), 0)
        query_at = keys - ROWS + lax.broadcasted_iota(jnp.int32, (1, ROWS), 1)
        allowed = (key_at <= query_at) & (key_at >= begin_of(query_at, first, second))
        bias[:keys] = jnp.where(allowed, 0.0, NEGATIVE)

        def some_heads(step, carry):
            def stack(ref):
                parts = [ref[at, lanes(step * HEADS + i, HD)] for i in range(HEADS)]
                return jnp.concatenate(parts, axis=0)

            query, grad = stack(q), stack(go)
            key, value = kv[:keys, :HD], kv[:keys, HD:]
            s = lax.dot_general(key, query, contract, preferred_element_type=F32)
            s = s + jnp.concatenate([bias[:keys]] * HEADS, axis=1)
            top = jnp.max(s, axis=0, keepdims=True)
            e = jnp.exp2((s - top) * (scale * LOG2E))
            share = 1.0 / jnp.sum(e, axis=0, keepdims=True)
            low = (e * share).astype(BF)
            attended = jnp.dot(vt[:, :keys], low, preferred_element_type=F32)
            delta = jnp.sum(attended * grad.astype(F32).T, axis=0, keepdims=True)
            dw = lax.dot_general(value, grad, contract, preferred_element_type=F32)
            ds = (e * share * (dw - delta)).astype(BF)
            dv_sum[:keys] += jnp.dot(low, grad, preferred_element_type=F32)
            dk_sum[:keys] += jnp.dot(ds, query, preferred_element_type=F32)
            turned = jnp.dot(kt[:, :keys], ds, preferred_element_type=F32)
            for i in range(HEADS):
                part = turned[:, i * ROWS : (i + 1) * ROWS].T * scale
                dq[at, lanes(step * HEADS + i, HD)] = part.astype(BF)
            return carry

        lax.fori_loop(0, 8 // HEADS, some_heads, 0, unroll=1)

    blocks = 512 // ROWS
    for half in range(2):
        for block in range(blocks):
            keys = (half * blocks + block + 1) * ROWS
            pl.when(u == half)(functools.partial(work, block, keys))
    dkv[:, :HD] = (dk_sum[...] * scale).astype(BF)
    dkv[:, HD:] = dv_sum[...].astype(BF)


def attend(lengths, q_h, go_h, kv_h):
    shape = jax.ShapeDtypeStruct
    return pl.pallas_call(
        attend_kernel,
        in_specs=[pl.BlockSpec(memory_space=pltpu.SMEM), VMEM, VMEM, VMEM],
        out_specs=[VMEM, VMEM],
        scratch_shapes=[
            pltpu.VMEM((1024, ROWS), F32),
            pltpu.VMEM((HD, 1024), BF),
            pltpu.VMEM((HD, 1024), BF),
            pltpu.VMEM((1024, HD), F32),
            pltpu.VMEM((1024, HD), F32),
        ],
        out_shape=[shape((512, 1024), BF), shape((1024, 256), BF)],
        compiler_params=pltpu.CompilerParams(vmem_limit_bytes=56 << 20),
    )(lengths, q_h, go_h, kv_h)


def backward_kernel(
    dkv, dq_h, hid_in, wk_in, wv_in, cosine, sine,
    dq, dhidden, grad_key, grad_value,
    send, recv, here, came, rows, hid, turned, wk, wv, dh, mine, low, away, other,
    key_in, value_in, key_sum, value_sum, key_last, value_last,
):
    p = Peers()
    u, x, z, w, c = p.u, p.x, p.z, p.w, p.c
    cp = Copies(send, recv)
    used = [0]

    def move(src, dst):
        copy = pltpu.make_async_copy(src, dst, here.at[used[0]])
        used[0] += 1
        copy.start()
        return copy

    hid_load = move(hid_in, hid)
    first = move(dkv.at[u, x], came.at[u, x])
    weight_loads = [move(wk_in, wk), move(wv_in, wv)]
    later = [move(dq_h.at[x], dq.at[:, lanes(x, 1024)])]
    meet(
        [p.along_z(d) for d in STEPS]
        + [p.on_plane(dy, dx) for dy, dx in PLANE]
        + [p.sibling()]
    )
    across = [
        cp.make(dkv.at[0, (x + dx) % 4], came.at[1, x], p.in_group(1, dx))
        for dx in (2, 1, 3, 0)
    ]

    @pl.when(u == 1)
    def _():
        for one in across:
            one.start()
        came[0] = jnp.zeros((4, TOK, 256), BF)

    pieces = [
        cp.start(dkv.at[u, (x + dx) % 4], came.at[u, x], p.along_x(dx)) for dx in STEPS
    ]
    hid_load.wait()

    def transpose(k, carry):
        block = hid[:, :, lanes(k, 128)].reshape(512, 128)
        turned[k] = block.astype(F32).T.astype(BF)
        return carry

    lax.fori_loop(0, 16, transpose, 0)
    first.wait()
    for one in pieces:
        one.wait_recv()

    @pl.when(u == 0)
    def _():
        for one in across:
            one.wait_recv()

    @pl.when(u == 1)
    def _():
        for one in across:
            one.wait_send()

    cos, sin = cosine[...], sine[...]
    for h in range(KV_HEADS):
        total = came[0, h].astype(F32) + came[1, h].astype(F32)
        dk = total[:, :HD]
        rows[z, :, h * HD : (h + 1) * HD] = (dk * cos - turn(dk) * sin).astype(BF)
        rows[z, :, 512 + h * HD : 512 + (h + 1) * HD] = total[:, HD:].astype(BF)
    sent_z = [cp.start(rows.at[z], rows.at[z], p.along_z(d)) for d in STEPS]
    sent = [
        cp.start(dq_h.at[(x + d) % 4], dq.at[:, lanes(x, 1024)], p.along_x(d)) for d in STEPS
    ]
    for one in weight_loads:
        one.wait()
    contract = (((1,), (1,)), ((), ()))

    def hidden_rows(slot, number):
        def one(piece, carry):
            key = wk[piece // 4, piece % 4].reshape(256, 512)
            value = wv[piece // 4, piece % 4].reshape(256, 512)
            total = lax.dot_general(
                rows[slot, :, :512], key, contract, preferred_element_type=F32
            ) + lax.dot_general(rows[slot, :, 512:], value, contract, preferred_element_type=F32)
            dh[number, :, lanes(piece, 256)] = total.astype(BF)
            return carry

        lax.fori_loop(0, 8, one, 0)

    hidden_rows(z, 3)
    for piece in range(8):
        later.append(
            move(
                dh.at[3, :, pl.ds(piece * 256, 256)],
                dhidden.at[:, lanes(piece * 4 + z, 256)],
            )
        )
    whole = []
    for number, d in enumerate(STEPS):
        slot = (z + 4 - d) % 4
        sent_z[number].wait_recv()
        hidden_rows(slot, number)
        at = cp.used
        for piece in range(8):
            cp.used = at
            cp.start(
                dh.at[number, :, pl.ds(piece * 256, 256)],
                dhidden.at[:, lanes(piece * 4 + z, 256)],
                p.along_z(4 - d),
            )
        cp.used = at
        whole.append(cp.make(dh.at[number], dh.at[number], p.along_z(4 - d)))
    order = PLANE + [(0, 0)]
    y = 2 * u + w
    swapped, key_out, value_out = [], {}, {}

    def pass_on(k):
        swapped[k].wait_recv()
        low[k] = (mine[k] + other[k].astype(F32)).astype(BF)
        dy, dx = order[k]
        if dx:
            key_out[dy, dx] = cp.start(
                low.at[k, :, pl.ds(0, 512)], key_in.at[dx - 1, (y + dy) % 4], p.along_x(dx)
            )
        if dy:
            value_out[dy, dx] = cp.start(
                low.at[k, :, pl.ds(512, 512)], value_in.at[dy - 1, (x + dx) % 4], p.along_y(dy)
            )

    for k, (dy, dx) in enumerate(order):
        tu, tw = p.y_at(dy)
        block = (tu * 4 + (x + dx) % 4) * 2 + tw
        product = jnp.dot(
            turned[block], rows[...].reshape(512, 1024), preferred_element_type=F32
        )
        zero_core = c == 0
        mine[k] = jnp.where(zero_core, product[:64], product[64:])
        away[k] = jnp.where(zero_core, product[64:], product[:64]).astype(BF)
        swapped.append(cp.start(away.at[k], other.at[k], p.sibling()))
        if k >= 2:
            pass_on(k - 2)
    pass_on(14)
    pass_on(15)
    last = []
    for d in (2, 1, 3, 0):
        for one in range(1, 4):
            key_out[d, one].wait_recv()
        at = order.index((d, 0))
        total = low[at, :, :512].astype(F32)
        for one in range(3):
            total = total + key_in[one, (y + d) % 4].astype(F32)
        if d:
            key_sum[d - 1] = total.astype(BF)
            last.append(cp.start(key_sum.at[d - 1], key_last.at[d - 1], p.along_y(d)))
        else:
            grad_key[...] = total
        for one in range(1, 4):
            value_out[one, d].wait_recv()
        at = order.index((0, d))
        total = low[at, :, 512:].astype(F32)
        for one in range(3):
            total = total + value_in[one, (x + d) % 4].astype(F32)
        if d:
            value_sum[d - 1] = total.astype(BF)
            last.append(cp.start(value_sum.at[d - 1], value_last.at[d - 1], p.along_x(d)))
        else:
            grad_value[...] = total
    for one in last:
        one.wait_recv()
    for one in range(3):
        grad_key[...] += key_last[one].astype(F32)
        grad_value[...] += value_last[one].astype(F32)
    out = list(key_out.values()) + list(value_out.values()) + last
    for one in whole + sent:
        one.wait_recv()
    for one in pieces + sent_z + sent + whole + swapped + out:
        one.wait_send()
    for one in later:
        one.wait()


def backward(dkv, dq_h, hid_g, wk, wv, cosine, sine):
    shape = jax.ShapeDtypeStruct
    weights = (2, 4, 2, 2, 64, 512)
    return comm_call(
        backward_kernel,
        1,
        (
            shape((TOK, 4096), BF),
            shape((TOK, WIDE), BF),
            shape((64, 512), F32),
            shape((64, 512), F32),
        ),
        [ANY] * 5 + [VMEM] * 2,
        (ANY, ANY, VMEM, VMEM),
        7 + 3 + 3 + 3 + 16 + 12 + 12 + 6,
        13,
        (
            pltpu.VMEM((2, 4, TOK, 256), BF),
            pltpu.VMEM((4, TOK, 1024), BF),
            pltpu.VMEM((4, TOK, 2048), BF),
            pltpu.VMEM((16, TOK, 512), BF),
            pltpu.VMEM(weights, BF),
            pltpu.VMEM(weights, BF),
            pltpu.VMEM((4, TOK, 2048), BF),
            pltpu.VMEM((16, 64, 1024), F32),
            pltpu.VMEM((16, 64, 1024), BF),
            pltpu.VMEM((16, 64, 1024), BF),
            pltpu.VMEM((16, 64, 1024), BF),
            pltpu.VMEM((3, 4, 64, 512), BF),
            pltpu.VMEM((3, 4, 64, 512), BF),
            *[pltpu.VMEM((3, 64, 512), BF)] * 4,
        ),
    )(dkv, dq_h, hid_g, wk, wv, cosine, sine)


PARTS = 4


def hand_on_kernel(*refs):
    count = (len(refs) - 2) // 3
    ins, outs, kept = refs[:count], refs[count : 2 * count], refs[2 * count : 3 * count]
    come, go = refs[-2:]
    loads, stores = [], []
    for i in range(count):
        size = ins[i].shape[0] // PARTS
        for j in range(PARTS):
            rows, at = pl.ds(j * size, size), i * PARTS + j
            loads.append(pltpu.make_async_copy(ins[i].at[rows], kept[i].at[rows], come.at[at]))
            stores.append(pltpu.make_async_copy(kept[i].at[rows], outs[i].at[rows], go.at[at]))
    for one in loads:
        one.start()
    for load, store in zip(loads, stores):
        load.wait()
        store.start()
    for one in stores:
        one.wait()


def hand_on(*arrays):
    count = len(arrays)
    return pl.pallas_call(
        hand_on_kernel,
        out_shape=[jax.ShapeDtypeStruct(one.shape, one.dtype) for one in arrays],
        in_specs=[ANY] * count,
        out_specs=[ANY] * count,
        scratch_shapes=[
            *[pltpu.VMEM(one.shape, one.dtype) for one in arrays],
            pltpu.SemaphoreType.DMA((count * PARTS,)),
            pltpu.SemaphoreType.DMA((count * PARTS,)),
        ],
    )(*arrays)


def local(hidden, queries, grad_out, key_weight, value_weight, doc_lengths):
    hid_g, wk, wv, q_h, go_h, kv_h, cosine, sine = forward(
        hidden[0], queries[0], grad_out[0], key_weight, value_weight, doc_lengths
    )
    dq_h, dkv = attend(
        doc_lengths, q_h.reshape(512, 1024), go_h.reshape(512, 1024), kv_h.reshape(1024, 256)
    )
    dquery, dhidden, grad_key, grad_value = hand_on(
        *backward(
            dkv.reshape(2, 4, TOK, 256), dq_h.reshape(4, TOK, 1024), hid_g, wk, wv, cosine, sine
        )
    )
    return dquery[None], dhidden[None], grad_key, grad_value


def solution(mesh):
    return jax.shard_map(
        local,
        mesh=mesh,
        in_specs=(
            P("dp", "zero", None),
            P("dp", "zero", None),
            P("dp", "zero", None),
            P(("zero", "dp"), None),
            P(("zero", "dp"), None),
            P("dp", None),
        ),
        out_specs=(
            P("dp", "zero", None),
            P("dp", "zero", None),
            P(("zero", "dp"), None),
            P(("zero", "dp"), None),
        ),
        check_vma=False,
    )
```

```python
import functools

import jax
import jax.numpy as jnp
import numpy as np
from jax import lax
from jax.experimental import pallas as pl
from jax.experimental.pallas import tpu as pltpu
from jax.sharding import PartitionSpec as P

KV_HEADS = 4
HD = 128
ROPE_BASE = 500000.0
NEGATIVE = -1e30
LOG2E = 1.4426950408889634
MESH = pl.DeviceIdType.MESH
TOK = 128
WIDE = 8192
ANY = pl.BlockSpec(memory_space=pl.ANY)
VMEM = pl.BlockSpec(memory_space=pltpu.VMEM)
BF = jnp.bfloat16
F32 = jnp.float32


FREQUENCY = (ROPE_BASE ** (-2.0 * (np.arange(HD) % (HD // 2)) / HD)).astype(np.float32)


def begin_of(at, first, second):
    return jnp.where(at >= second, second, jnp.where(at >= first, first, 0))


def place():
    j, i = lax.axis_index("zero"), lax.axis_index("dp")
    return j // 4, j % 4, i // 4, (i // 2) % 2, i % 2


def device(u, x, z, w, c):
    return (u * 4 + x, z * 4 + w * 2 + c)


class Peers:
    def __init__(self):
        self.u, self.x, self.z, self.w, self.c = place()

    def along_x(self, d):
        return device(self.u, (self.x + d) % 4, self.z, self.w, self.c)

    def along_z(self, d):
        return device(self.u, self.x, (self.z + d) % 4, self.w, self.c)

    def y_at(self, d):
        y = (2 * self.u + self.w + d) % 4
        return y // 2, y % 2

    def along_y(self, d):
        u, w = self.y_at(d)
        return device(u, self.x, self.z, w, self.c)

    def in_group(self, du, dx):
        return device((self.u + du) % 2, (self.x + dx) % 4, self.z, self.w, self.c)

    def on_plane(self, dy, dx):
        u, w = self.y_at(dy)
        return device(u, (self.x + dx) % 4, self.z, w, self.c)

    def sibling(self):
        return device(self.u, self.x, self.z, self.w, 1 - self.c)


def meet(devices):
    barrier = pltpu.get_barrier_semaphore()
    for one in devices:
        pl.semaphore_signal(barrier, inc=1, device_id=one, device_id_type=MESH)
    pl.semaphore_wait(barrier, len(devices))


class Copies:
    def __init__(self, send, recv):
        self.send, self.recv, self.used = send, recv, 0

    def make(self, src, dst, to):
        at = self.used
        self.used += 1
        return pltpu.make_async_remote_copy(
            src_ref=src,
            dst_ref=dst,
            send_sem=self.send.at[at],
            recv_sem=self.recv.at[at],
            device_id=to,
            device_id_type=MESH,
        )

    def start(self, src, dst, to):
        copy = self.make(src, dst, to)
        copy.start()
        return copy


GROUP = [(du, dx) for du in (1, 0) for dx in (2, 1, 3, 0)][:-1]
PLANE = [(dy, dx) for dy in (2, 1, 3, 0) for dx in (2, 1, 3, 0)][:-1]
STEPS = (1, 3, 2)


def comm_call(kernel, number, outs, in_specs, out_specs, remote, local, scratch=()):
    return pl.pallas_call(
        kernel,
        out_shape=outs,
        in_specs=in_specs,
        out_specs=out_specs,
        scratch_shapes=[
            pltpu.SemaphoreType.DMA((remote,)),
            pltpu.SemaphoreType.DMA((remote,)),
            pltpu.SemaphoreType.DMA((local,)),
            *scratch,
        ],
        compiler_params=pltpu.CompilerParams(
            collective_id=number, has_side_effects=True, vmem_limit_bytes=63 << 20
        ),
    )


def lanes(at, size):
    return pl.ds(pl.multiple_of(at * size, size), size)


def turn(rows):
    return pltpu.roll(rows, HD // 2, 1)


WEIGHTS = (2, 4, 2, 2, 64, 512)
CONTRACT = (((1,), (1,)), ((), ()))


def whole_kernel(
    hidden, query, grad, wkey, wvalue, frequency, lengths,
    dq, dhidden, grad_key, grad_value,
    send, recv, here,
    hid, wk, wv, k_part, v_part, k_in, v_in, k_own, v_own, k_rows, v_rows,
    q_h, go_h, k_h, v_h, kt, vt, bias, ex, share, dk_sum, dv_sum, dk_out, dv_out, dq_h,
    k_came, v_came, rows_k, rows_v, turned, dh, low, away, other,
    key_in, value_in, key_sum, value_sum, key_last, value_last,
):
    p = Peers()
    u, x, z, w, c = p.u, p.x, p.z, p.w, p.c
    cp = Copies(send, recv)
    used = [0]
    scale = HD**-0.5
    first_end, second_end = lengths[0, 0], lengths[0, 0] + lengths[0, 1]

    def move(src, dst):
        copy = pltpu.make_async_copy(src, dst, here.at[used[0]])
        used[0] += 1
        copy.start()
        return copy

    own_key = move(wkey, wk.at[u, x, w, c])
    own_value = move(wvalue, wv.at[u, x, w, c])
    own_hidden = [
        move(hidden.at[:, lanes(piece * 4 + z, 256)], hid.at[z, :, pl.ds(piece * 256, 256)])
        for piece in range(8)
    ]
    own_heads = [
        move(query.at[:, lanes(x, 1024)], q_h.at[x]),
        move(grad.at[:, lanes(x, 1024)], go_h.at[x]),
    ]
    meet(
        [p.along_z(d) for d in STEPS]
        + [p.on_plane(dy, dx) for dy, dx in PLANE]
        + [p.sibling()]
    )
    key_y = [cp.start(wkey, wk.at[u, x, w, c], p.along_y(d)) for d in STEPS]
    value_x = [cp.start(wvalue, wv.at[u, x, w, c], p.along_x(d)) for d in STEPS]
    whole = []
    for d in STEPS:
        there, at = (z + d) % 4, cp.used
        for piece in range(8):
            cp.used = at
            cp.start(
                hidden.at[:, lanes(piece * 4 + there, 256)],
                hid.at[z, :, pl.ds(piece * 256, 256)],
                p.along_z(d),
            )
        cp.used = at
        came = (z + 4 - d) % 4
        whole.append(cp.make(hid.at[came], hid.at[came], p.along_z(d)))
    at = (u * 4 + x) * TOK + lax.broadcasted_iota(jnp.int32, (TOK, HD), 0)
    angles = (at - begin_of(at, first_end, second_end)).astype(F32) * frequency[...]
    sign = jnp.where(lax.broadcasted_iota(jnp.int32, (TOK, HD), 1) < HD // 2, -1.0, 1.0)
    cos, sin = jnp.cos(angles), sign * jnp.sin(angles)
    dk_sum[...] = jnp.zeros_like(dk_sum)
    dv_sum[...] = jnp.zeros_like(dv_sum)

    @pl.when(u == 0)
    def _():
        k_h[1] = jnp.zeros((4, TOK, HD), BF)
        v_h[1] = jnp.zeros((4, TOK, HD), BF)

    @pl.when(u == 1)
    def _():
        k_came[0] = jnp.zeros((4, TOK, HD), BF)
        v_came[0] = jnp.zeros((4, TOK, HD), BF)

    own_key.wait()
    for one in key_y:
        one.wait_recv()
    column = wk.at[:, x, :, c]
    key_x = [cp.start(column, column, p.along_x(d)) for d in STEPS]
    to_core = [cp.start(column, column, p.sibling())]
    own_value.wait()
    for one in value_x:
        one.wait_recv()
    row = wv.at[u, :, w, c]
    value_y = [cp.start(row, row, p.along_y(d)) for d in STEPS]
    to_core.append(cp.start(row, row, p.sibling()))
    sent_heads = []
    for source, target in ((query, q_h), (grad, go_h)):
        for d in STEPS:
            sent_heads.append(
                cp.start(source.at[:, lanes((x + d) % 4, 1024)], target.at[x], p.along_x(d))
            )
    for d, one in zip(STEPS, key_x):
        one.wait_recv()
        column = wk.at[:, (x + 4 - d) % 4, :, c]
        to_core.append(cp.start(column, column, p.sibling()))
    for d, one in zip(STEPS, value_y):
        one.wait_recv()
        from_u, from_w = p.y_at(4 - d)
        row = wv.at[from_u, :, from_w, c]
        to_core.append(cp.start(row, row, p.sibling()))
    for one in own_hidden:
        one.wait()
    for one in to_core:
        one.wait_recv()

    def project(slot, weights):
        return jnp.dot(hid[slot], weights[...].reshape(2048, 512), preferred_element_type=F32)

    k_own[...] = project(z, wk)
    k_back, v_back = [], []
    for number, d in enumerate(STEPS):
        whole[number].wait_recv()
        k_part[number] = project((z + 4 - d) % 4, wk)
        k_back.append(cp.start(k_part.at[number], k_in.at[number], p.along_z(4 - d)))
    for number, d in enumerate(STEPS):
        v_part[number] = project((z + 4 - d) % 4, wv).astype(BF)
        v_back.append(cp.start(v_part.at[number], v_in.at[number], p.along_z(4 - d)))
    v_own[...] = project(z, wv)

    def transpose(k, carry):
        block = hid[:, :, lanes(k, 128)].reshape(512, 128)
        turned[k] = block.astype(F32).T.astype(BF)
        return carry

    lax.fori_loop(0, 16, transpose, 0)

    def exchange(source, target, low_to_high):
        across = [cp.make(source(dx, 1), target.at[u, x], p.in_group(1, dx)) for dx in (2, 1, 3, 0)]

        @pl.when(u == (0 if low_to_high else 1))
        def _():
            for one in across:
                one.start()

        own = move(source(0, 0), target.at[u, x])
        near = [cp.start(source(dx, 0), target.at[u, x], p.along_x(dx)) for dx in STEPS]

        def receive():
            own.wait()
            for one in near:
                one.wait_recv()

            @pl.when(u == (1 if low_to_high else 0))
            def _():
                for one in across:
                    one.wait_recv()

        def sent():
            for one in near:
                one.wait_send()

            @pl.when(u == (0 if low_to_high else 1))
            def _():
                for one in across:
                    one.wait_send()

        return receive, sent

    def head_of(rows):
        return lambda dx, du: rows.at[:, lanes((x + dx) % 4, HD)]

    def owner_of(rows):
        return lambda dx, du: rows.at[0 if du else u, (x + dx) % 4]

    for one in k_back:
        one.wait_recv()
    for h in range(KV_HEADS):
        part = slice(h * HD, (h + 1) * HD)
        k = k_own[:, part]
        for number in range(3):
            k = k + k_in[number, :, part]
        k_rows[:, part] = (k * cos + turn(k) * sin).astype(BF)
    receive_k, sent_k = exchange(head_of(k_rows), k_h, True)
    for one in own_heads:
        one.wait()
    for one in sent_heads:
        one.wait_recv()
    receive_k()
    kt[...] = k_h[...].reshape(1024, HD).astype(F32).T.astype(BF)

    def stack(ref, block):
        parts = [ref[block, :, h * HD : (h + 1) * HD] for h in range(8)]
        return jnp.concatenate(parts, axis=0)

    def either(work, block):
        for half in range(2):
            pl.when(u == half)(functools.partial(work, block, (half * 4 + block + 1) * TOK))

    def weigh(block, keys):
        key_at = lax.broadcasted_iota(jnp.int32, (keys, TOK), 0)
        query_at = keys - TOK + lax.broadcasted_iota(jnp.int32, (1, TOK), 1)
        allowed = (key_at <= query_at) & (key_at >= begin_of(query_at, first_end, second_end))
        bias[:keys] = jnp.where(allowed, 0.0, NEGATIVE)
        key = k_h[...].reshape(1024, HD)[:keys]
        s = lax.dot_general(key, stack(q_h, block), CONTRACT, preferred_element_type=F32)
        s = s + jnp.concatenate([bias[:keys]] * 8, axis=1)
        top = jnp.max(s, axis=0, keepdims=True)
        e = jnp.exp2((s - top) * (scale * LOG2E))
        ex[block, :keys] = e
        inverse = 1.0 / jnp.sum(e, axis=0, keepdims=True)
        share[block, 0:1] = inverse
        weights = (e * inverse).astype(BF)
        dv_sum[:keys] += jnp.dot(weights, stack(go_h, block), preferred_element_type=F32)

    def differentiate(block, keys):
        grads = stack(go_h, block)
        value = v_h[...].reshape(1024, HD)[:keys]
        inverse = share[block, 0:1]
        weights = ex[block, :keys] * inverse
        attended = jnp.dot(vt[:, :keys], weights.astype(BF), preferred_element_type=F32)
        delta = jnp.sum(attended * grads.astype(F32).T, axis=0, keepdims=True)
        dw = lax.dot_general(value, grads, CONTRACT, preferred_element_type=F32)
        ds = (weights * (dw - delta)).astype(BF)
        dk_sum[:keys] += jnp.dot(ds, stack(q_h, block), preferred_element_type=F32)
        back = jnp.dot(kt[:, :keys], ds, preferred_element_type=F32)
        for h in range(8):
            part = back[:, h * TOK : (h + 1) * TOK].T * scale
            dq_h[block, :, h * HD : (h + 1) * HD] = part.astype(BF)

    either(weigh, 0)
    either(weigh, 1)
    for one in v_back:
        one.wait_recv()
    v = v_own[...]
    for number in range(3):
        v = v + v_in[number].astype(F32)
    v_rows[...] = v.astype(BF)
    receive_v, sent_v = exchange(head_of(v_rows), v_h, True)
    either(weigh, 2)
    either(weigh, 3)
    dv_out[...] = dv_sum[...].astype(BF).reshape(2, 4, TOK, HD)
    receive_dv, sent_dv = exchange(owner_of(dv_out), v_came, False)
    receive_v()
    vt[...] = v_h[...].reshape(1024, HD).astype(F32).T.astype(BF)
    either(differentiate, 0)
    either(differentiate, 1)
    receive_dv()
    for h in range(KV_HEADS):
        total = v_came[0, h].astype(F32) + v_came[1, h].astype(F32)
        rows_v[z, :, h * HD : (h + 1) * HD] = total.astype(BF)
    sent_z = [cp.start(rows_v.at[z], rows_v.at[z], p.along_z(d)) for d in STEPS]
    either(differentiate, 2)
    either(differentiate, 3)
    dk_out[...] = (dk_sum[...] * scale).astype(BF).reshape(2, 4, TOK, HD)
    receive_dk, sent_dk = exchange(owner_of(dk_out), k_came, False)
    later = [move(dq_h.at[x], dq.at[:, lanes(x, 1024)])]
    receive_dk()
    for h in range(KV_HEADS):
        dk = k_came[0, h].astype(F32) + k_came[1, h].astype(F32)
        rows_k[z, :, h * HD : (h + 1) * HD] = (dk * cos - turn(dk) * sin).astype(BF)
    sent_zk = [cp.start(rows_k.at[z], rows_k.at[z], p.along_z(d)) for d in STEPS]
    sent = [
        cp.start(dq_h.at[(x + d) % 4], dq.at[:, lanes(x, 1024)], p.along_x(d)) for d in STEPS
    ]

    def hidden_rows(slot, number):
        def one(piece, carry):
            key = wk[piece // 4, piece % 4].reshape(256, 512)
            value = wv[piece // 4, piece % 4].reshape(256, 512)
            total = lax.dot_general(
                rows_k[slot], key, CONTRACT, preferred_element_type=F32
            ) + lax.dot_general(rows_v[slot], value, CONTRACT, preferred_element_type=F32)
            dh[number, :, lanes(piece, 256)] = total.astype(BF)
            return carry

        lax.fori_loop(0, 8, one, 0)

    hidden_rows(z, 3)
    for piece in range(8):
        later.append(
            move(dh.at[3, :, pl.ds(piece * 256, 256)], dhidden.at[:, lanes(piece * 4 + z, 256)])
        )
    returned = []
    for number, d in enumerate(STEPS):
        sent_z[number].wait_recv()
        sent_zk[number].wait_recv()
        hidden_rows((z + 4 - d) % 4, number)
        at = cp.used
        for piece in range(8):
            cp.used = at
            cp.start(
                dh.at[number, :, pl.ds(piece * 256, 256)],
                dhidden.at[:, lanes(piece * 4 + z, 256)],
                p.along_z(4 - d),
            )
        cp.used = at
        returned.append(cp.make(dh.at[number], dh.at[number], p.along_z(4 - d)))
    order = PLANE + [(0, 0)]
    swapped, key_out, value_out = [], {}, {}

    def mine(k):
        return ex.at[0, pl.ds(k * 64, 64)]

    def pass_on(k):
        swapped[k].wait_recv()
        low[k] = (mine(k)[...] + other[k].astype(F32)).astype(BF)
        dy, dx = order[k]
        if dx:
            key_out[dy, dx] = cp.start(
                low.at[k, :, pl.ds(0, 512)],
                key_in.at[dx - 1, (2 * u + w + dy) % 4],
                p.along_x(dx),
            )
        if dy:
            value_out[dy, dx] = cp.start(
                low.at[k, :, pl.ds(512, 512)], value_in.at[dy - 1, (x + dx) % 4], p.along_y(dy)
            )

    for k, (dy, dx) in enumerate(order):
        tu, tw = p.y_at(dy)
        block = (tu * 4 + (x + dx) % 4) * 2 + tw
        for lane, rows in ((0, rows_k), (512, rows_v)):
            product = jnp.dot(
                turned[block], rows[...].reshape(512, 512), preferred_element_type=F32
            )
            kept = jnp.where(c == 0, product[:64], product[64:])
            given = jnp.where(c == 0, product[64:], product[:64])
            mine(k)[:, lane : lane + 512] = kept
            away[k, :, lane : lane + 512] = given.astype(BF)
        swapped.append(cp.start(away.at[k], other.at[k], p.sibling()))
        if k >= 2:
            pass_on(k - 2)
    pass_on(14)
    pass_on(15)
    last = []
    for d in (2, 1, 3, 0):
        for one in range(1, 4):
            key_out[d, one].wait_recv()
        total = low[order.index((d, 0)), :, :512].astype(F32)
        for one in range(3):
            total = total + key_in[one, (2 * u + w + d) % 4].astype(F32)
        if d:
            key_sum[d - 1] = total.astype(BF)
            last.append(cp.start(key_sum.at[d - 1], key_last.at[d - 1], p.along_y(d)))
        else:
            grad_key[...] = total
        for one in range(1, 4):
            value_out[one, d].wait_recv()
        total = low[order.index((0, d)), :, 512:].astype(F32)
        for one in range(3):
            total = total + value_in[one, (x + d) % 4].astype(F32)
        if d:
            value_sum[d - 1] = total.astype(BF)
            last.append(cp.start(value_sum.at[d - 1], value_last.at[d - 1], p.along_x(d)))
        else:
            grad_value[...] = total
    for one in last:
        one.wait_recv()
    for one in range(3):
        grad_key[...] += key_last[one].astype(F32)
        grad_value[...] += value_last[one].astype(F32)
    for one in returned + sent:
        one.wait_recv()
    for one in (sent_k, sent_v, sent_dv, sent_dk):
        one()
    for group in (
        key_y, value_x, whole, key_x, value_y, to_core, sent_heads, k_back, v_back,
        sent_z, sent_zk, sent, returned, swapped, key_out.values(), value_out.values(), last,
    ):
        for one in group:
            one.wait_send()
    for one in later:
        one.wait()


def whole_layer(hidden, query, grad, wkey, wvalue, lengths):
    shape, vmem = jax.ShapeDtypeStruct, pltpu.VMEM
    return comm_call(
        whole_kernel,
        0,
        (
            shape((TOK, 4096), BF),
            shape((TOK, WIDE), BF),
            shape((64, 512), F32),
            shape((64, 512), F32),
        ),
        [ANY] * 5 + [VMEM, pl.BlockSpec(memory_space=pltpu.SMEM)],
        (ANY, ANY, VMEM, VMEM),
        124,
        28,
        (
            vmem((4, TOK, 2048), BF),
            vmem(WEIGHTS, BF),
            vmem(WEIGHTS, BF),
            vmem((3, TOK, 512), F32),
            vmem((3, TOK, 512), BF),
            vmem((3, TOK, 512), F32),
            vmem((3, TOK, 512), BF),
            vmem((TOK, 512), F32),
            vmem((TOK, 512), F32),
            vmem((TOK, 512), BF),
            vmem((TOK, 512), BF),
            vmem((4, TOK, 1024), BF),
            vmem((4, TOK, 1024), BF),
            vmem((2, 4, TOK, HD), BF),
            vmem((2, 4, TOK, HD), BF),
            vmem((HD, 1024), BF),
            vmem((HD, 1024), BF),
            vmem((1024, TOK), F32),
            vmem((4, 1024, 1024), F32),
            vmem((4, 8, 1024), F32),
            vmem((1024, HD), F32),
            vmem((1024, HD), F32),
            vmem((2, 4, TOK, HD), BF),
            vmem((2, 4, TOK, HD), BF),
            vmem((4, TOK, 1024), BF),
            vmem((2, 4, TOK, HD), BF),
            vmem((2, 4, TOK, HD), BF),
            vmem((4, TOK, 512), BF),
            vmem((4, TOK, 512), BF),
            vmem((16, TOK, 512), BF),
            vmem((4, TOK, 2048), BF),
            vmem((16, 64, 1024), BF),
            vmem((16, 64, 1024), BF),
            vmem((16, 64, 1024), BF),
            vmem((3, 4, 64, 512), BF),
            vmem((3, 4, 64, 512), BF),
            *[vmem((3, 64, 512), BF)] * 4,
        ),
    )(hidden, query, grad, wkey, wvalue, jnp.asarray(FREQUENCY)[None], lengths)


PARTS = 4


def hand_on_kernel(*refs):
    count = (len(refs) - 2) // 3
    ins, outs, kept = refs[:count], refs[count : 2 * count], refs[2 * count : 3 * count]
    come, go = refs[-2:]
    loads, stores = [], []
    for i in range(count):
        size = ins[i].shape[0] // PARTS
        for j in range(PARTS):
            rows, at = pl.ds(j * size, size), i * PARTS + j
            loads.append(pltpu.make_async_copy(ins[i].at[rows], kept[i].at[rows], come.at[at]))
            stores.append(pltpu.make_async_copy(kept[i].at[rows], outs[i].at[rows], go.at[at]))
    for one in loads:
        one.start()
    for load, store in zip(loads, stores):
        load.wait()
        store.start()
    for one in stores:
        one.wait()


def hand_on(*arrays):
    count = len(arrays)
    return pl.pallas_call(
        hand_on_kernel,
        out_shape=[jax.ShapeDtypeStruct(one.shape, one.dtype) for one in arrays],
        in_specs=[ANY] * count,
        out_specs=[ANY] * count,
        scratch_shapes=[
            *[pltpu.VMEM(one.shape, one.dtype) for one in arrays],
            pltpu.SemaphoreType.DMA((count * PARTS,)),
            pltpu.SemaphoreType.DMA((count * PARTS,)),
        ],
    )(*arrays)


def local(hidden, queries, grad_out, key_weight, value_weight, doc_lengths):
    dquery, dhidden, grad_key, grad_value = hand_on(
        *whole_layer(
            hidden[0], queries[0], grad_out[0], key_weight, value_weight, doc_lengths
        )
    )
    return dquery[None], dhidden[None], grad_key, grad_value


def solution(mesh):
    return jax.shard_map(
        local,
        mesh=mesh,
        in_specs=(
            P("dp", "zero", None),
            P("dp", "zero", None),
            P("dp", "zero", None),
            P(("zero", "dp"), None),
            P(("zero", "dp"), None),
            P("dp", None),
        ),
        out_specs=(
            P("dp", "zero", None),
            P("dp", "zero", None),
            P(("zero", "dp"), None),
            P(("zero", "dp"), None),
        ),
        check_vma=False,
    )
```

```python
import functools

import jax
import jax.numpy as jnp
import numpy as np
from jax import lax
from jax.experimental import pallas as pl
from jax.experimental.pallas import tpu as pltpu
from jax.sharding import PartitionSpec as P

KV_HEADS = 4
HD = 128
ROPE_BASE = 500000.0
NEGATIVE = -1e30
LOG2E = 1.4426950408889634
MESH = pl.DeviceIdType.MESH
TOK = 128
WIDE = 8192
ANY = pl.BlockSpec(memory_space=pl.ANY)
VMEM = pl.BlockSpec(memory_space=pltpu.VMEM)
BF = jnp.bfloat16
F32 = jnp.float32


FREQUENCY = (ROPE_BASE ** (-2.0 * (np.arange(HD) % (HD // 2)) / HD)).astype(np.float32)


def begin_of(at, first, second):
    return jnp.where(at >= second, second, jnp.where(at >= first, first, 0))


def place():
    j, i = lax.axis_index("zero"), lax.axis_index("dp")
    return j // 4, j % 4, i // 4, (i // 2) % 2, i % 2


def device(u, x, z, w, c):
    return (u * 4 + x, z * 4 + w * 2 + c)


class Peers:
    def __init__(self):
        self.u, self.x, self.z, self.w, self.c = place()

    def along_x(self, d):
        return device(self.u, (self.x + d) % 4, self.z, self.w, self.c)

    def along_z(self, d):
        return device(self.u, self.x, (self.z + d) % 4, self.w, self.c)

    def y_at(self, d):
        y = (2 * self.u + self.w + d) % 4
        return y // 2, y % 2

    def along_y(self, d):
        u, w = self.y_at(d)
        return device(u, self.x, self.z, w, self.c)

    def in_group(self, du, dx):
        return device((self.u + du) % 2, (self.x + dx) % 4, self.z, self.w, self.c)

    def on_plane(self, dy, dx):
        u, w = self.y_at(dy)
        return device(u, (self.x + dx) % 4, self.z, w, self.c)

    def sibling(self):
        return device(self.u, self.x, self.z, self.w, 1 - self.c)


def meet(devices):
    barrier = pltpu.get_barrier_semaphore()
    for one in devices:
        pl.semaphore_signal(barrier, inc=1, device_id=one, device_id_type=MESH)
    pl.semaphore_wait(barrier, len(devices))


class Copies:
    def __init__(self, send, recv):
        self.send, self.recv, self.used = send, recv, 0

    def make(self, src, dst, to):
        at = self.used
        self.used += 1
        return pltpu.make_async_remote_copy(
            src_ref=src,
            dst_ref=dst,
            send_sem=self.send.at[at],
            recv_sem=self.recv.at[at],
            device_id=to,
            device_id_type=MESH,
        )

    def start(self, src, dst, to):
        copy = self.make(src, dst, to)
        copy.start()
        return copy


GROUP = [(du, dx) for du in (1, 0) for dx in (2, 1, 3, 0)][:-1]
PLANE = [(dy, dx) for dy in (2, 1, 3, 0) for dx in (2, 1, 3, 0)][:-1]
STEPS = (1, 3, 2)


def comm_call(kernel, number, outs, in_specs, out_specs, remote, local, scratch=()):
    return pl.pallas_call(
        kernel,
        out_shape=outs,
        in_specs=in_specs,
        out_specs=out_specs,
        scratch_shapes=[
            pltpu.SemaphoreType.DMA((remote,)),
            pltpu.SemaphoreType.DMA((remote,)),
            pltpu.SemaphoreType.DMA((local,)),
            *scratch,
        ],
        compiler_params=pltpu.CompilerParams(
            collective_id=number, has_side_effects=True, vmem_limit_bytes=63 << 20
        ),
    )


def lanes(at, size):
    return pl.ds(pl.multiple_of(at * size, size), size)


def turn(rows):
    return pltpu.roll(rows, HD // 2, 1)


WEIGHTS = (2, 4, 2, 2, 64, 512)
CONTRACT = (((1,), (1,)), ((), ()))


def whole_kernel(
    hidden, query, grad, wkey, wvalue, frequency, lengths,
    dq, dhidden, grad_key, grad_value,
    send, recv, here,
    hid, wk, wv, k_part, v_part, k_in, v_in, k_own, v_own, k_rows, v_rows,
    q_h, go_h, k_h, v_h, kt, vt, bias, ex, share, dk_sum, dv_sum, dk_out, dv_out, dq_h,
    k_came, v_came, rows_k, rows_v, turned, dh, low, away, other,
    key_in, value_in, key_sum, value_sum, key_last, value_last,
):
    p = Peers()
    u, x, z, w, c = p.u, p.x, p.z, p.w, p.c
    cp = Copies(send, recv)
    used = [0]
    scale = HD**-0.5
    first_end, second_end = lengths[0, 0], lengths[0, 0] + lengths[0, 1]

    def move(src, dst):
        copy = pltpu.make_async_copy(src, dst, here.at[used[0]])
        used[0] += 1
        copy.start()
        return copy

    barrier = pltpu.get_barrier_semaphore()
    met = (
        [p.along_z(d) for d in STEPS]
        + [p.on_plane(dy, dx) for dy, dx in PLANE]
        + [p.sibling()]
    )
    for one in met:
        pl.semaphore_signal(barrier, inc=1, device_id=one, device_id_type=MESH)
    own_key = move(wkey, wk.at[u, x, w, c])
    own_value = move(wvalue, wv.at[u, x, w, c])
    own_hidden = [
        move(hidden.at[:, lanes(piece * 4 + z, 256)], hid.at[z, :, pl.ds(piece * 256, 256)])
        for piece in range(8)
    ]
    own_heads = [
        move(query.at[:, lanes(x, 1024)], q_h.at[x]),
        move(grad.at[:, lanes(x, 1024)], go_h.at[x]),
    ]
    pl.semaphore_wait(barrier, len(met))
    key_y = [cp.start(wkey, wk.at[u, x, w, c], p.along_y(d)) for d in STEPS]
    value_x = [cp.start(wvalue, wv.at[u, x, w, c], p.along_x(d)) for d in STEPS]
    whole = []
    for d in STEPS:
        there, at = (z + d) % 4, cp.used
        for piece in range(8):
            cp.used = at
            cp.start(
                hidden.at[:, lanes(piece * 4 + there, 256)],
                hid.at[z, :, pl.ds(piece * 256, 256)],
                p.along_z(d),
            )
        cp.used = at
        came = (z + 4 - d) % 4
        whole.append(cp.make(hid.at[came], hid.at[came], p.along_z(d)))
    at = (u * 4 + x) * TOK + lax.broadcasted_iota(jnp.int32, (TOK, HD), 0)
    angles = (at - begin_of(at, first_end, second_end)).astype(F32) * frequency[...]
    sign = jnp.where(lax.broadcasted_iota(jnp.int32, (TOK, HD), 1) < HD // 2, -1.0, 1.0)
    cos, sin = jnp.cos(angles), sign * jnp.sin(angles)
    dk_sum[...] = jnp.zeros_like(dk_sum)
    dv_sum[...] = jnp.zeros_like(dv_sum)

    @pl.when(u == 0)
    def _():
        k_h[1] = jnp.zeros((4, TOK, HD), BF)
        v_h[1] = jnp.zeros((4, TOK, HD), BF)

    @pl.when(u == 1)
    def _():
        k_came[0] = jnp.zeros((4, TOK, HD), BF)
        v_came[0] = jnp.zeros((4, TOK, HD), BF)

    own_key.wait()
    for one in key_y:
        one.wait_recv()
    column = wk.at[:, x, :, c]
    key_x = [cp.start(column, column, p.along_x(d)) for d in STEPS]
    to_core = [cp.start(column, column, p.sibling())]
    own_value.wait()
    for one in value_x:
        one.wait_recv()
    row = wv.at[u, :, w, c]
    value_y = [cp.start(row, row, p.along_y(d)) for d in STEPS]
    to_core.append(cp.start(row, row, p.sibling()))
    sent_heads = []
    for source, target in ((query, q_h), (grad, go_h)):
        for d in STEPS:
            sent_heads.append(
                cp.start(source.at[:, lanes((x + d) % 4, 1024)], target.at[x], p.along_x(d))
            )
    for d, one in zip(STEPS, key_x):
        one.wait_recv()
        column = wk.at[:, (x + 4 - d) % 4, :, c]
        to_core.append(cp.start(column, column, p.sibling()))
    for d, one in zip(STEPS, value_y):
        one.wait_recv()
        from_u, from_w = p.y_at(4 - d)
        row = wv.at[from_u, :, from_w, c]
        to_core.append(cp.start(row, row, p.sibling()))
    for one in own_hidden:
        one.wait()
    for one in to_core:
        one.wait_recv()

    def project(slot, weights):
        return jnp.dot(hid[slot], weights[...].reshape(2048, 512), preferred_element_type=F32)

    k_own[...] = project(z, wk)
    k_back, v_back = [], []
    for number, d in enumerate(STEPS):
        whole[number].wait_recv()
        k_part[number] = project((z + 4 - d) % 4, wk)
        k_back.append(cp.start(k_part.at[number], k_in.at[number], p.along_z(4 - d)))
    for number, d in enumerate(STEPS):
        v_part[number] = project((z + 4 - d) % 4, wv).astype(BF)
        v_back.append(cp.make(v_part.at[number], v_in.at[number], p.along_z(4 - d)))
    v_own[...] = project(z, wv)

    def transpose(k, carry):
        block = hid[:, :, lanes(k, 128)].reshape(512, 128)
        turned[k] = block.astype(F32).T.astype(BF)
        return carry

    lax.fori_loop(0, 16, transpose, 0)

    def exchange(source, target, low_to_high):
        across = [cp.make(source(dx, 1), target.at[u, x], p.in_group(1, dx)) for dx in (2, 1, 3, 0)]

        @pl.when(u == (0 if low_to_high else 1))
        def _():
            for one in across:
                one.start()

        own = move(source(0, 0), target.at[u, x])
        near = [cp.start(source(dx, 0), target.at[u, x], p.along_x(dx)) for dx in STEPS]

        def receive():
            own.wait()
            for one in near:
                one.wait_recv()

            @pl.when(u == (1 if low_to_high else 0))
            def _():
                for one in across:
                    one.wait_recv()

        def sent():
            for one in near:
                one.wait_send()

            @pl.when(u == (0 if low_to_high else 1))
            def _():
                for one in across:
                    one.wait_send()

        return receive, sent

    def head_of(rows):
        return lambda dx, du: rows.at[:, lanes((x + dx) % 4, HD)]

    def owner_of(rows):
        return lambda dx, du: rows.at[0 if du else u, (x + dx) % 4]

    for one in k_back:
        one.wait_recv()
    for h in range(KV_HEADS):
        part = slice(h * HD, (h + 1) * HD)
        k = k_own[:, part]
        for number in range(3):
            k = k + k_in[number, :, part]
        k_rows[:, part] = (k * cos + turn(k) * sin).astype(BF)
    receive_k, sent_k = exchange(head_of(k_rows), k_h, True)
    for one in v_back:
        one.start()
    for one in own_heads:
        one.wait()
    for one in sent_heads:
        one.wait_recv()
    receive_k()
    kt[...] = k_h[...].reshape(1024, HD).astype(F32).T.astype(BF)

    def stack(ref, block):
        parts = [ref[block, :, h * HD : (h + 1) * HD] for h in range(8)]
        return jnp.concatenate(parts, axis=0)

    def either(work, block):
        for half in range(2):
            pl.when(u == half)(functools.partial(work, block, (half * 4 + block + 1) * TOK))

    def weigh(block, keys):
        key_at = lax.broadcasted_iota(jnp.int32, (keys, TOK), 0)
        query_at = keys - TOK + lax.broadcasted_iota(jnp.int32, (1, TOK), 1)
        allowed = (key_at <= query_at) & (key_at >= begin_of(query_at, first_end, second_end))
        bias[:keys] = jnp.where(allowed, 0.0, NEGATIVE)
        key = k_h[...].reshape(1024, HD)[:keys]
        s = lax.dot_general(key, stack(q_h, block), CONTRACT, preferred_element_type=F32)
        s = s + jnp.concatenate([bias[:keys]] * 8, axis=1)
        top = jnp.max(s, axis=0, keepdims=True)
        e = jnp.exp2((s - top) * (scale * LOG2E))
        ex[block, :keys] = e
        inverse = 1.0 / jnp.sum(e, axis=0, keepdims=True)
        share[block, 0:1] = inverse
        weights = (e * inverse).astype(BF)
        dv_sum[:keys] += jnp.dot(weights, stack(go_h, block), preferred_element_type=F32)

    def differentiate(block, keys):
        grads = stack(go_h, block)
        value = v_h[...].reshape(1024, HD)[:keys]
        inverse = share[block, 0:1]
        weights = ex[block, :keys] * inverse
        attended = jnp.dot(vt[:, :keys], weights.astype(BF), preferred_element_type=F32)
        delta = jnp.sum(attended * grads.astype(F32).T, axis=0, keepdims=True)
        dw = lax.dot_general(value, grads, CONTRACT, preferred_element_type=F32)
        ds = (weights * (dw - delta)).astype(BF)
        dk_sum[:keys] += jnp.dot(ds, stack(q_h, block), preferred_element_type=F32)
        back = jnp.dot(kt[:, :keys], ds, preferred_element_type=F32)
        for h in range(8):
            part = back[:, h * TOK : (h + 1) * TOK].T * scale
            dq_h[block, :, h * HD : (h + 1) * HD] = part.astype(BF)

    either(weigh, 0)
    either(weigh, 1)
    for one in v_back:
        one.wait_recv()
    v = v_own[...]
    for number in range(3):
        v = v + v_in[number].astype(F32)
    v_rows[...] = v.astype(BF)
    receive_v, sent_v = exchange(head_of(v_rows), v_h, True)
    either(weigh, 2)
    either(weigh, 3)
    dv_out[...] = dv_sum[...].astype(BF).reshape(2, 4, TOK, HD)
    receive_dv, sent_dv = exchange(owner_of(dv_out), v_came, False)
    receive_v()
    vt[...] = v_h[...].reshape(1024, HD).astype(F32).T.astype(BF)
    either(differentiate, 0)
    either(differentiate, 1)
    receive_dv()
    for h in range(KV_HEADS):
        total = v_came[0, h].astype(F32) + v_came[1, h].astype(F32)
        rows_v[z, :, h * HD : (h + 1) * HD] = total.astype(BF)
    sent_z = [cp.start(rows_v.at[z], rows_v.at[z], p.along_z(d)) for d in STEPS]
    either(differentiate, 2)
    either(differentiate, 3)
    dk_out[...] = (dk_sum[...] * scale).astype(BF).reshape(2, 4, TOK, HD)
    receive_dk, sent_dk = exchange(owner_of(dk_out), k_came, False)
    later = [move(dq_h.at[x], dq.at[:, lanes(x, 1024)])]
    receive_dk()
    for h in range(KV_HEADS):
        dk = k_came[0, h].astype(F32) + k_came[1, h].astype(F32)
        rows_k[z, :, h * HD : (h + 1) * HD] = (dk * cos - turn(dk) * sin).astype(BF)
    sent_zk = [cp.start(rows_k.at[z], rows_k.at[z], p.along_z(d)) for d in STEPS]
    sent = [
        cp.start(dq_h.at[(x + d) % 4], dq.at[:, lanes(x, 1024)], p.along_x(d)) for d in STEPS
    ]

    def hidden_rows(slot, number):
        def one(piece, carry):
            key = wk[piece // 4, piece % 4].reshape(256, 512)
            value = wv[piece // 4, piece % 4].reshape(256, 512)
            total = lax.dot_general(
                rows_k[slot], key, CONTRACT, preferred_element_type=F32
            ) + lax.dot_general(rows_v[slot], value, CONTRACT, preferred_element_type=F32)
            dh[number, :, lanes(piece, 256)] = total.astype(BF)
            return carry

        lax.fori_loop(0, 8, one, 0)

    hidden_rows(z, 3)
    for piece in range(8):
        later.append(
            move(dh.at[3, :, pl.ds(piece * 256, 256)], dhidden.at[:, lanes(piece * 4 + z, 256)])
        )
    returned = []
    for number, d in enumerate(STEPS):
        sent_z[number].wait_recv()
        sent_zk[number].wait_recv()
        hidden_rows((z + 4 - d) % 4, number)
        at = cp.used
        for piece in range(8):
            cp.used = at
            cp.start(
                dh.at[number, :, pl.ds(piece * 256, 256)],
                dhidden.at[:, lanes(piece * 4 + z, 256)],
                p.along_z(4 - d),
            )
        cp.used = at
        returned.append(cp.make(dh.at[number], dh.at[number], p.along_z(4 - d)))
    order = PLANE + [(0, 0)]
    swapped, key_out, value_out = [], {}, {}

    def mine(k):
        return ex.at[0, pl.ds(k * 64, 64)]

    def pass_on(k):
        swapped[k].wait_recv()
        low[k] = (mine(k)[...] + other[k].astype(F32)).astype(BF)
        dy, dx = order[k]
        if dx:
            key_out[dy, dx] = cp.start(
                low.at[k, :, pl.ds(0, 512)],
                key_in.at[dx - 1, (2 * u + w + dy) % 4],
                p.along_x(dx),
            )
        if dy:
            value_out[dy, dx] = cp.start(
                low.at[k, :, pl.ds(512, 512)], value_in.at[dy - 1, (x + dx) % 4], p.along_y(dy)
            )

    for k, (dy, dx) in enumerate(order):
        tu, tw = p.y_at(dy)
        block = (tu * 4 + (x + dx) % 4) * 2 + tw
        for lane, rows in ((0, rows_k), (512, rows_v)):
            product = jnp.dot(
                turned[block], rows[...].reshape(512, 512), preferred_element_type=F32
            )
            kept = jnp.where(c == 0, product[:64], product[64:])
            given = jnp.where(c == 0, product[64:], product[:64])
            mine(k)[:, lane : lane + 512] = kept
            away[k, :, lane : lane + 512] = given.astype(BF)
        swapped.append(cp.start(away.at[k], other.at[k], p.sibling()))
        if k >= 2:
            pass_on(k - 2)
    pass_on(14)
    pass_on(15)
    last = []
    for d in (2, 1, 3, 0):
        for one in range(1, 4):
            key_out[d, one].wait_recv()
        total = low[order.index((d, 0)), :, :512].astype(F32)
        for one in range(3):
            total = total + key_in[one, (2 * u + w + d) % 4].astype(F32)
        if d:
            key_sum[d - 1] = total.astype(BF)
            last.append(cp.start(key_sum.at[d - 1], key_last.at[d - 1], p.along_y(d)))
        else:
            grad_key[...] = total
        for one in range(1, 4):
            value_out[one, d].wait_recv()
        total = low[order.index((0, d)), :, 512:].astype(F32)
        for one in range(3):
            total = total + value_in[one, (x + d) % 4].astype(F32)
        if d:
            value_sum[d - 1] = total.astype(BF)
            last.append(cp.start(value_sum.at[d - 1], value_last.at[d - 1], p.along_x(d)))
        else:
            grad_value[...] = total
    for one in last:
        one.wait_recv()
    for one in range(3):
        grad_key[...] += key_last[one].astype(F32)
        grad_value[...] += value_last[one].astype(F32)
    for one in returned + sent:
        one.wait_recv()
    for one in (sent_k, sent_v, sent_dv, sent_dk):
        one()
    for group in (
        key_y, value_x, whole, key_x, value_y, to_core, sent_heads, k_back, v_back,
        sent_z, sent_zk, sent, returned, swapped, key_out.values(), value_out.values(), last,
    ):
        for one in group:
            one.wait_send()
    for one in later:
        one.wait()


def whole_layer(hidden, query, grad, wkey, wvalue, lengths):
    shape, vmem = jax.ShapeDtypeStruct, pltpu.VMEM
    return comm_call(
        whole_kernel,
        0,
        (
            shape((TOK, 4096), BF),
            shape((TOK, WIDE), BF),
            shape((64, 512), F32),
            shape((64, 512), F32),
        ),
        [ANY] * 5 + [VMEM, pl.BlockSpec(memory_space=pltpu.SMEM)],
        (ANY, ANY, VMEM, VMEM),
        124,
        28,
        (
            vmem((4, TOK, 2048), BF),
            vmem(WEIGHTS, BF),
            vmem(WEIGHTS, BF),
            vmem((3, TOK, 512), F32),
            vmem((3, TOK, 512), BF),
            vmem((3, TOK, 512), F32),
            vmem((3, TOK, 512), BF),
            vmem((TOK, 512), F32),
            vmem((TOK, 512), F32),
            vmem((TOK, 512), BF),
            vmem((TOK, 512), BF),
            vmem((4, TOK, 1024), BF),
            vmem((4, TOK, 1024), BF),
            vmem((2, 4, TOK, HD), BF),
            vmem((2, 4, TOK, HD), BF),
            vmem((HD, 1024), BF),
            vmem((HD, 1024), BF),
            vmem((1024, TOK), F32),
            vmem((4, 1024, 1024), F32),
            vmem((4, 8, 1024), F32),
            vmem((1024, HD), F32),
            vmem((1024, HD), F32),
            vmem((2, 4, TOK, HD), BF),
            vmem((2, 4, TOK, HD), BF),
            vmem((4, TOK, 1024), BF),
            vmem((2, 4, TOK, HD), BF),
            vmem((2, 4, TOK, HD), BF),
            vmem((4, TOK, 512), BF),
            vmem((4, TOK, 512), BF),
            vmem((16, TOK, 512), BF),
            vmem((4, TOK, 2048), BF),
            vmem((16, 64, 1024), BF),
            vmem((16, 64, 1024), BF),
            vmem((16, 64, 1024), BF),
            vmem((3, 4, 64, 512), BF),
            vmem((3, 4, 64, 512), BF),
            *[vmem((3, 64, 512), BF)] * 4,
        ),
    )(hidden, query, grad, wkey, wvalue, jnp.asarray(FREQUENCY)[None], lengths)


PARTS = 4


def hand_on_kernel(*refs):
    count = (len(refs) - 2) // 3
    ins, outs, kept = refs[:count], refs[count : 2 * count], refs[2 * count : 3 * count]
    come, go = refs[-2:]
    loads, stores = [], []
    for i in range(count):
        size = ins[i].shape[0] // PARTS
        for j in range(PARTS):
            rows, at = pl.ds(j * size, size), i * PARTS + j
            loads.append(pltpu.make_async_copy(ins[i].at[rows], kept[i].at[rows], come.at[at]))
            stores.append(pltpu.make_async_copy(kept[i].at[rows], outs[i].at[rows], go.at[at]))
    for one in loads:
        one.start()
    for load, store in zip(loads, stores):
        load.wait()
        store.start()
    for one in stores:
        one.wait()


def hand_on(*arrays):
    count = len(arrays)
    return pl.pallas_call(
        hand_on_kernel,
        out_shape=[jax.ShapeDtypeStruct(one.shape, one.dtype) for one in arrays],
        in_specs=[ANY] * count,
        out_specs=[ANY] * count,
        scratch_shapes=[
            *[pltpu.VMEM(one.shape, one.dtype) for one in arrays],
            pltpu.SemaphoreType.DMA((count * PARTS,)),
            pltpu.SemaphoreType.DMA((count * PARTS,)),
        ],
    )(*arrays)


def local(hidden, queries, grad_out, key_weight, value_weight, doc_lengths):
    dquery, dhidden, grad_key, grad_value = hand_on(
        *whole_layer(
            hidden[0], queries[0], grad_out[0], key_weight, value_weight, doc_lengths
        )
    )
    return dquery[None], dhidden[None], grad_key, grad_value


def solution(mesh):
    return jax.shard_map(
        local,
        mesh=mesh,
        in_specs=(
            P("dp", "zero", None),
            P("dp", "zero", None),
            P("dp", "zero", None),
            P(("zero", "dp"), None),
            P(("zero", "dp"), None),
            P("dp", None),
        ),
        out_specs=(
            P("dp", "zero", None),
            P("dp", "zero", None),
            P(("zero", "dp"), None),
            P(("zero", "dp"), None),
        ),
        check_vma=False,
    )
```
